32 devices in a mesh: gx: 8 (over z, y), gy: 4 (over x, core).
Axes of the slice: x: 2, y: 2, z: 4, core: 2. Of those that a mesh axis runs over, the one named last changes fastest.
Arguments:
- state: float32 [148, 256, 1024], P(None, 'gy', 'gx'), may hold values from -8 to 8
- wind: float32 [2, 37, 256, 1024], P(None, None, 'gy', 'gx'), may hold values from -0.8 to 0.8
- forcing: bfloat16 [148, 256, 1024], P(None, 'gy', 'gx'), may hold values from -6 to 6
- zone: int32 [256, 1024], P('gy', 'gx'), may hold values from 0 to 5
- land: int32 [256, 1024], P('gy', 'gx'), may hold values 0 or 1
- terrain: int32 [256, 1024], P('gy', 'gx'), may hold values from 0 to 7
- first_weight: bfloat16 [9, 256, 148], replicated, may hold values from -0.15625 to 0.15625
- second_weight: bfloat16 [256, 256], replicated, may hold values from -0.375 to 0.375
- third_weight: bfloat16 [148, 256], replicated, may hold values from -0.0625 to 0.0625
- land_embed: bfloat16 [256, 2], replicated, may hold values from -3 to 3
- terrain_embed: bfloat16 [256, 8], replicated, may hold values from -3 to 3
Outputs:
- updated: float32 [148, 256, 1024], P(None, 'gy', 'gx')
The draws below stay inside these ranges and needn't reach their ends.
All inputs are finite; a program needn't handle non-finite values. No bound on the sum of `land` on one device may be relied on, other than what follows from the above.
Results may differ from the reference program's by a relative error of at most 0.00036.
Values may be sent and summed in bfloat16 or wider, within the bound.
No kernel may reach another device: no remote copies, remote signals or barrier semaphores. Data moves between devices by JAX's collectives and lax.ppermute only.
A program may use at most 256 MiB of HBM per device.

```python
import math
import jax
import jax.numpy as jnp
from jax import lax

VARS = 4
LEV = 37
FEAT = 148
UNITS = 256
TERRAIN = 8
NY = 256
NX = 1024


def draw_state(key, part):
    key = jax.random.fold_in(key, 7)
    rough_key, scale_key = jax.random.split(key)
    row_ids = jnp.arange(NY, dtype=jnp.int32)[:, None]
    col_ids = jnp.arange(NX, dtype=jnp.int32)[None, :]
    checker = (1 - 2 * ((row_ids + col_ids) % 2)).astype(jnp.float32)
    rough_part = jax.random.truncated_normal(rough_key, -5.0, 5.0, (FEAT, NY, NX), jnp.float32)
    amplitude = jax.random.uniform(scale_key, (FEAT, 1, 1), jnp.float32, 1.0, 2.0)
    return rough_part + amplitude * checker[None, :, :]


def draw_wind(key, part):
    key = jax.random.fold_in(key, 11)
    sign_key, speed_key = jax.random.split(key)
    signs = (2 * jax.random.randint(sign_key, (2, LEV, 1, 1), 0, 2) - 1).astype(jnp.float32)
    speed = jax.random.uniform(speed_key, (2, LEV, NY, NX), jnp.float32, 0.6, 0.8)
    return signs * speed


def plant(values, key, least, largest):
    spot = [jax.random.randint(jax.random.fold_in(key, axis), (), 0, length) for axis, length in enumerate(values.shape)]
    main_axis = values.shape.index(max(values.shape))
    neighbour = spot[:main_axis] + [(spot[main_axis] + 1) % values.shape[main_axis]] + spot[main_axis + 1:]
    return values.at[tuple(spot)].set(least).at[tuple(neighbour)].set(largest)


def steps_of(rng, extent, cuts, least, top_value):
    loudness, own = 1.0, jax.random.fold_in(rng, 6)
    for position, parts in cuts:
        steps = jnp.exp(jax.random.uniform(jax.random.fold_in(own, position), (parts,), jnp.float32, least / len(cuts), top_value / len(cuts)))
        loudness = loudness * jnp.repeat(steps, extent[position] // parts).reshape([-1 if axis == position else 1 for axis in range(len(extent))])
    return loudness


def normal_values(own_key, extent, width, limit, cuts=(), kind=jnp.bfloat16):
    array = width * jax.random.normal(own_key, extent, jnp.float32)
    if cuts:
        array = array * steps_of(own_key, extent, cuts, -0.22, 0.18)
    return jnp.clip(array, -limit, limit).astype(kind)


def setup_inputs(seed: int = 0) -> dict:
    key_of = jax.random.split(jax.random.key(seed), 12)
    state = draw_state(jax.random.fold_in(key_of[11], 71), 0)
    wind = draw_wind(jax.random.fold_in(key_of[11], 71), 0)
    forcing = normal_values(key_of[2], (FEAT, NY, NX), 1.0, 6.0, ((1, 4), (2, 8)))
    zone = plant(jax.random.randint(key_of[3], (NY, NX), 0, 6), jax.random.fold_in(key_of[3], 1), 0, 5).astype(jnp.int32)
    land = plant((jax.random.randint(key_of[4], (NY, NX), 0, 3) < 1).astype(jnp.int32), jax.random.fold_in(key_of[4], 1), 0, 1)
    terrain = plant(jax.random.randint(key_of[5], (NY, NX), 0, TERRAIN), jax.random.fold_in(key_of[5], 1), 0, TERRAIN - 1).astype(jnp.int32)
    first_weight = normal_values(key_of[6], (9, UNITS, FEAT), (9 * FEAT) ** -0.5, 0.15625)
    second_weight = normal_values(key_of[7], (UNITS, UNITS), UNITS ** -0.5, 0.375)
    third_weight = normal_values(key_of[8], (FEAT, UNITS), (36 * UNITS) ** -0.5, 0.0625)
    land_embed = normal_values(key_of[9], (UNITS, 2), 0.5, 3.0)
    terrain_embed = normal_values(key_of[10], (UNITS, TERRAIN), 0.5, 3.0)
    return dict(state=state, wind=wind, forcing=forcing, zone=zone, land=land, terrain=terrain, first_weight=first_weight, second_weight=second_weight, third_weight=third_weight, land_embed=land_embed, terrain_embed=terrain_embed)


DIFFUSION = 0.1
RELAX_STEP = 0.1
ONE_THIRD = 1.0 / 3.0
TWO_THIRDS = 2.0 / 3.0


def tendency(padded, wind_part):
    center = padded[..., 1:-1, 1:-1]
    east = padded[..., 1:-1, 2:]
    west = padded[..., 1:-1, :-2]
    north = padded[..., 2:, 1:-1]
    south = padded[..., :-2, 1:-1]
    along_x = (east - west) * 0.5
    along_y = (north - south) * 0.5
    laplace = east + west + north + south - 4.0 * center
    return DIFFUSION * laplace - (wind_part[0] * along_x + wind_part[1] * along_y)


def pad_plane(field):
    return jnp.pad(field, ((0, 0), (1, 1), (1, 1)))


def mlp_rest(hidden_pre, second_weight, third_weight):
    first_act = jax.nn.silu(hidden_pre).astype(jnp.bfloat16)
    second_pre = jnp.dot(second_weight, first_act, preferred_element_type=jnp.float32)
    second_act = jax.nn.silu(second_pre).astype(jnp.bfloat16)
    return jnp.dot(third_weight, second_act, preferred_element_type=jnp.float32)


def reference(state, wind, forcing, zone, land, terrain, first_weight, second_weight, third_weight, land_embed, terrain_embed):
    weight_relax = zone.astype(jnp.float32) * RELAX_STEP

    def dycore_var(values):
        level_state, forcing_var = values
        first = level_state + tendency(pad_plane(level_state), wind)
        second = 0.75 * level_state + 0.25 * (first + tendency(pad_plane(first), wind))
        third = ONE_THIRD * level_state + TWO_THIRDS * (second + tendency(pad_plane(second), wind))
        return third + weight_relax * (forcing_var.astype(jnp.float32) - third)

    relaxed = lax.map(dycore_var, (state.reshape(VARS, LEV, NY, NX), forcing.reshape(VARS, LEV, NY, NX)))
    relaxed = relaxed.reshape(FEAT, NY, NX)
    column_in = relaxed.astype(jnp.bfloat16)
    padded = jnp.pad(column_in, ((0, 0), (1, 1), (1, 1)))
    block = math.gcd(NY, 16)
    count = NY // block

    def one_block(index):
        start = (index * block).astype(jnp.int32)
        window = lax.dynamic_slice_in_dim(padded, start, block + 2, 1)
        land_rows = lax.dynamic_slice_in_dim(land, start, block, 0).reshape(1, block * NX)
        terrain_rows = lax.dynamic_slice_in_dim(terrain, start, block, 0).reshape(1, block * NX)
        land_hot = (land_rows == jnp.arange(2, dtype=jnp.int32)[:, None]).astype(jnp.bfloat16)
        terrain_hot = (terrain_rows == jnp.arange(TERRAIN, dtype=jnp.int32)[:, None]).astype(jnp.bfloat16)
        hidden_pre = jnp.dot(land_embed, land_hot, preferred_element_type=jnp.float32)
        hidden_pre = hidden_pre + jnp.dot(terrain_embed, terrain_hot, preferred_element_type=jnp.float32)
        for row_off in range(3):
            for col_off in range(3):
                piece = window[:, row_off:row_off + block, col_off:col_off + NX].reshape(FEAT, block * NX)
                hidden_pre = hidden_pre + jnp.dot(first_weight[row_off * 3 + col_off], piece, preferred_element_type=jnp.float32)
        return mlp_rest(hidden_pre, second_weight, third_weight).reshape(FEAT, block, NX)

    blocks = lax.map(one_block, jnp.arange(count, dtype=jnp.int32))
    physics = blocks.transpose(1, 0, 2, 3).reshape(FEAT, NY, NX)
    return relaxed + physics
```

```python
import jax
import jax.numpy as jnp
from jax import lax
from jax.experimental import pallas as pl
from jax.experimental.pallas import tpu as pltpu
from jax.sharding import PartitionSpec as P

F32, BF16 = jnp.float32, jnp.bfloat16
V, L, F, R, C = 4, 37, 148, 64, 128
LQ = 10
E = 72
BW, BF, BZ, BN = 592, 888, 1036, 1048
PITCH = 158
KP = 160
LIM = 60 << 20
THIRD = 1.0 / 3.0


def iota(shape, dim):
    return lax.broadcasted_iota(jnp.int32, shape, dim)


def ns_pack(s0, s7, w0, w7, f0, f3, z0, z7, down, up):
    for f in range(F):
        down[f * 4 : f * 4 + 4, :] = s0[f, 0:4, :]
        up[f * 4 : f * 4 + 4, :] = s7[f, 4:8, :]
    for w in range(2 * L):
        down[BW + w * 4 : BW + w * 4 + 4, :] = w0[w, 0:4, :]
        up[BW + w * 4 : BW + w * 4 + 4, :] = w7[w, 4:8, :]
    for f in range(F):
        down[BF + f : BF + f + 1, :] = f0[f].astype(F32)[0:1]
        up[BF + f : BF + f + 1, :] = f3[f].astype(F32)[15:16]
    down[BZ : BZ + 8, :] = z0[...].astype(F32) * 0.1
    zu = z7[...].astype(F32) * 0.1
    up[BZ : BZ + 1, :] = zu[7:8]
    up[BZ + 1 : BN, :] = jnp.zeros((BN - BZ - 1, C), F32)
    down[BZ + 8 : BN, :] = jnp.zeros((BN - BZ - 8, C), F32)


def pack_north_south(state, wind, forcing, zone):
    st = jax.ShapeDtypeStruct((BN, C), F32)
    full = pl.BlockSpec((BN, C), lambda i: (0, 0))
    return pl.pallas_call(
        ns_pack,
        grid=(1,),
        out_shape=(st, st),
        in_specs=[
            pl.BlockSpec((F, 8, C), lambda i: (0, 0, 0)),
            pl.BlockSpec((F, 8, C), lambda i: (0, 7, 0)),
            pl.BlockSpec((2 * L, 8, C), lambda i: (0, 0, 0)),
            pl.BlockSpec((2 * L, 8, C), lambda i: (0, 7, 0)),
            pl.BlockSpec((F, 16, C), lambda i: (0, 0, 0)),
            pl.BlockSpec((F, 16, C), lambda i: (0, 3, 0)),
            pl.BlockSpec((8, C), lambda i: (0, 0)),
            pl.BlockSpec((8, C), lambda i: (7, 0)),
        ],
        out_specs=(full, full),
        compiler_params=pltpu.CompilerParams(vmem_limit_bytes=LIM),
        name="ns_pack",
    )(state, state, wind, wind, forcing, forcing, zone, zone)


def selector(j, ring):
    lane = iota((C, C), 1)
    col = iota((C, C), 0)
    pos = lane % 32
    if ring:
        want = jnp.where(pos == 11, 127, jnp.where(pos == 20, 0, -1))
    else:
        want = jnp.where(pos < 12, 116 + pos, jnp.where(pos >= 20, pos - 20, -1))
    return jnp.where((want == col) & (lane // 32 == j), 1.0, 0.0).astype(BF16)


def split(x):
    hi = x.astype(BF16)
    lo = (x - hi.astype(F32)).astype(BF16)
    return hi, lo


def ew_pack(state, wind, forcing, zone, below, above, strips, wstrips, east, west, sel, rsel):
    lg = pl.program_id(0)
    lane = iota((E, C), 1) % 32

    @pl.when(lg == 0)
    def _():
        for j in range(4):
            s = selector(j, False)
            sel[2 * j * C : (2 * j + 1) * C, :] = s
            sel[(2 * j + 1) * C : (2 * j + 2) * C, :] = s
            rsel[j * C : (j + 1) * C, :] = selector(j, True)
        east[5:9] = jnp.zeros((4, E, C), F32)
        west[5:9] = jnp.zeros((4, E, C), F32)
        zed = jnp.concatenate(
            [
                zone[...].astype(F32) * 0.1,
                above[BZ : BZ + 1, :],
                jnp.zeros((6, C), F32),
                below[BZ : BZ + 1, :],
            ],
            axis=0,
        )
        zlane = pltpu.roll(zed, 20, 1)
        z0 = jnp.where(iota((E, C), 1) == 20, zlane, 0.0)
        z127 = jnp.where(iota((E, C), 1) == 20, pltpu.roll(zed, 21, 1), 0.0)
        for ref, val in ((east, z127), (west, z0)):
            tot = jnp.zeros((E, C), F32)
            for j in range(4):
                tot = tot + pltpu.roll(val, (j * 32 + 8 - 20) % C, 1)
            ref[8] = tot

    def ext(main, base, i, rows):
        return jnp.concatenate(
            [main, above[pl.ds(base + i * rows, rows), :], below[pl.ds(base + i * rows, rows), :]], axis=0
        )

    def clean(x, level):
        return x if level < 5 else jnp.where(lg * 8 + level < L, x, 0.0)

    def clamp(level):
        return jnp.minimum(lg * 8 + level, L - 1)

    for m in range(2):
        lq = lg * 2 + m
        for v in range(V):
            parts, ring = [], []
            for j in range(4):
                i = m * 4 + j
                x = clean(ext(state[v, i], 0, v * L + clamp(i), 4), i)
                parts += list(split(x))
                fmain = forcing[v, i].astype(F32)
                fv = jnp.concatenate(
                    [
                        fmain,
                        above[pl.ds(BF + v * L + clamp(i), 1), :],
                        jnp.zeros((6, C), F32),
                        below[pl.ds(BF + v * L + clamp(i), 1), :],
                    ],
                    axis=0,
                )
                ring.append(clean(fv, i).astype(BF16))
            s = jnp.dot(jnp.concatenate(parts, axis=1), sel[...], preferred_element_type=F32)
            strips[m, v] = s
            q = m * 4 + v
            put = (lane >= q * 4) & (lane < q * 4 + 4)
            e = pltpu.roll(s, (q * 4 - 8) % C, 1)
            w = pltpu.roll(s, (q * 4 - 20) % C, 1)
            if q == 0:
                east[lg] = jnp.where(put, e, 0.0)
                west[lg] = jnp.where(put, w, 0.0)
            else:
                east[lg] = jnp.where(put, e, east[lg])
                west[lg] = jnp.where(put, w, west[lg])
            fs = jnp.dot(jnp.concatenate(ring, axis=1), rsel[...], preferred_element_type=F32)
            pk = 7 + lg // 4
            qq = (lg % 4) * 8 + q
            east[pk] = jnp.where(lane == qq, pltpu.roll(fs, (qq - 11 + C) % C, 1), east[pk])
            west[pk] = jnp.where(lane == qq, pltpu.roll(fs, (qq - 20 + C) % C, 1), west[pk])
        for c in range(2):
            parts = []
            for j in range(4):
                i = m * 4 + j
                parts += list(split(clean(ext(wind[c, i], BW, c * L + clamp(i), 4), i)))
            s = jnp.dot(jnp.concatenate(parts, axis=1), sel[...], preferred_element_type=F32)
            wstrips[m, c] = s
            put = (lane >= lq * 3) & (lane < lq * 3 + 3)
            east[5 + c] = jnp.where(put, pltpu.roll(s, (lq * 3 - 9 + C) % C, 1), east[5 + c])
            west[5 + c] = jnp.where(put, pltpu.roll(s, (lq * 3 - 20 + C) % C, 1), west[5 + c])


def pack_east_west(state, wind, forcing, zone, below, above):
    send = jax.ShapeDtypeStruct((9, E, C), F32)
    return pl.pallas_call(
        ew_pack,
        grid=(5,),
        out_shape=(
            jax.ShapeDtypeStruct((LQ, V, E, C), F32),
            jax.ShapeDtypeStruct((LQ, 2, E, C), F32),
            send,
            send,
        ),
        in_specs=[
            pl.BlockSpec((V, 8, R, C), lambda i: (0, i, 0, 0)),
            pl.BlockSpec((2, 8, R, C), lambda i: (0, i, 0, 0)),
            pl.BlockSpec((V, 8, R, C), lambda i: (0, i, 0, 0)),
            pl.BlockSpec((R, C), lambda i: (0, 0)),
            pl.BlockSpec((BN, C), lambda i: (0, 0)),
            pl.BlockSpec((BN, C), lambda i: (0, 0)),
        ],
        out_specs=(
            pl.BlockSpec((2, V, E, C), lambda i: (i, 0, 0, 0)),
            pl.BlockSpec((2, 2, E, C), lambda i: (i, 0, 0, 0)),
            pl.BlockSpec((9, E, C), lambda i: (0, 0, 0)),
            pl.BlockSpec((9, E, C), lambda i: (0, 0, 0)),
        ),
        scratch_shapes=[pltpu.VMEM((8 * C, C), BF16), pltpu.VMEM((4 * C, C), BF16)],
        compiler_params=pltpu.CompilerParams(vmem_limit_bytes=LIM),
        name="ew_pack",
    )(state, wind, forcing, zone, below, above)


def put_ring(ref, v, i, val):
    ref[v, 8 + i * 8 : 16 + i * 8, :] = val
    if i == 0:
        ref[v, 80:81, :] = val[0:1]
    if i == 8:
        ref[v, 7:8, :] = val[7:8]


def around(ref, v, i):
    q = ref[v, 8 + i * 8 : 16 + i * 8, :]
    n = ref[v, 9 + i * 8 : 17 + i * 8, :]
    s = ref[v, 7 + i * 8 : 15 + i * 8, :]
    return q, pltpu.roll(q, C - 1, 1), pltpu.roll(q, 1, 1), n, s


def stage_three(f2, c2, w2, emit):
    for i in range(9):
        rows = slice(i * 8, i * 8 + 8)
        ce, cw, cn, cs = (w2[k, rows, :] for k in range(4))
        for v in range(V):
            q, e, w, n, s = around(f2, v, i)
            g = (ce * e + cw * w) + (cn * n + cs * s)
            emit(v, i, THIRD * c2[v, rows, :] + (2.0 * THIRD) * (0.6 * q + g))


def stage_two(f1, c1, w1, f2, c2, w2):
    for i in range(9):
        rows = slice(i * 8, i * 8 + 8)
        ce, cw, cn, cs = (w1[k, rows, :] for k in range(4))
        for v in range(V):
            q, e, w, n, s = around(f1, v, i)
            g = (ce * e + cw * w) + (cn * n + cs * s)
            c = c1[v, rows, :]
            c2[v, rows, :] = c
            put_ring(f2, v, i, 0.75 * c + 0.25 * (0.6 * q + g))
        for k, val in enumerate((ce, cw, cn, cs)):
            w2[k, rows, :] = val


def stage_one(x, wind_at, diff, f1, c1, w1):
    for i in range(9):
        rows = slice(i * 8, i * 8 + 8)
        d = diff[rows, :]
        hu, hv = (0.5 * wind_at(k, i) for k in range(2))
        ce, cw, cn, cs = d - hu, d + hu, d - hv, d + hv
        for v in range(V):
            q, e, w, n, s = around(x, v, i)
            g = (ce * e + cw * w) + (cn * n + cs * s)
            c1[v, rows, :] = q
            put_ring(f1, v, i, 0.6 * q + g)
        for k, val in enumerate((ce, cw, cn, cs)):
            w1[k, rows, :] = val


def diffusion(strip):
    row, lane = iota((E, C), 0), iota((E, C), 1)
    gy, gx = lax.axis_index("gy"), lax.axis_index("gx")
    ok_above = jnp.where(gy < lax.axis_size("gy") - 1, 1, 0)
    ok_below = jnp.where(gy > 0, 1, 0)
    ok = jnp.where(row < 64, 1, jnp.where(row < 68, ok_above, ok_below))
    if strip:
        pos = lane % 32
        ok_east = jnp.where(gx < lax.axis_size("gx") - 1, 1, 0)
        ok_west = jnp.where(gx > 0, 1, 0)
        ok = ok * jnp.where((pos >= 12) & (pos < 16), ok_east, jnp.where((pos >= 16) & (pos < 20), ok_west, 1))
    return 0.1 * ok.astype(F32)


def stage_scratch():
    return [
        pltpu.VMEM((V, 88, C), F32),
        pltpu.VMEM((V, 88, C), F32),
        pltpu.VMEM((V, 88, C), F32),
        pltpu.VMEM((V, E, C), F32),
        pltpu.VMEM((V, E, C), F32),
        pltpu.VMEM((4, E, C), F32),
        pltpu.VMEM((4, E, C), F32),
        pltpu.VMEM((E, C), F32),
    ]


def main_stages(state, wind, below, above, third, x, f1, f2, c1, c2, w1, w2, diff):
    step = pl.program_id(0)

    @pl.when(step == 0)
    def _():
        diff[...] = diffusion(False)

    level = jnp.minimum(step, L - 1)

    def emit(v, i, val):
        third[v, 0, i * 8 : i * 8 + 8, :] = val

    stage_three(f2, c2, w2, emit)
    stage_two(f1, c1, w1, f2, c2, w2)
    for v in range(V):
        for i in range(8):
            put_ring(x, v, i, state[v, 0, i * 8 : i * 8 + 8, :])
        at = pl.ds((v * L + level) * 4, 4)
        put_ring(x, v, 8, jnp.concatenate([above[at, :], below[at, :]], axis=0))

    def wind_at(k, i):
        if i < 8:
            return wind[k, 0, i * 8 : i * 8 + 8, :]
        at = pl.ds(BW + (k * L + level) * 4, 4)
        return jnp.concatenate([above[at, :], below[at, :]], axis=0)

    stage_one(x, wind_at, diff, f1, c1, w1)


def run_main(state, wind, below, above):
    return pl.pallas_call(
        main_stages,
        grid=(L + 2,),
        out_shape=jax.ShapeDtypeStruct((V, L, E, C), F32),
        in_specs=[
            pl.BlockSpec((V, 1, R, C), lambda i: (0, jnp.minimum(i, L - 1), 0, 0)),
            pl.BlockSpec((2, 1, R, C), lambda i: (0, jnp.minimum(i, L - 1), 0, 0)),
            pl.BlockSpec((BN, C), lambda i: (0, 0)),
            pl.BlockSpec((BN, C), lambda i: (0, 0)),
        ],
        out_specs=pl.BlockSpec((V, 1, E, C), lambda i: (0, jnp.maximum(i - 2, 0), 0, 0)),
        scratch_shapes=stage_scratch(),
        compiler_params=pltpu.CompilerParams(vmem_limit_bytes=LIM),
        cost_estimate=pl.CostEstimate(flops=60_000_000, bytes_accessed=13_000_000, transcendentals=0),
        name="main_stages",
    )(state, wind, below, above)


def silu(v):
    h = 0.5 * v
    return h + h * jnp.tanh(h)


def last(
    third, strips, wstrips, fromw, frome, forcing, zone, land, terrain, below, above, wb, w2t, w3t,
    out,
    x, f1, f2, c1, c2, w1, w2, diff, sr, zs, zx, y0, ym, yp, b0, bm, bp,
):
    lane = iota((8, C), 1)
    pos = lane % 32
    diff[...] = diffusion(True)
    zx[0:64, :] = zone[...].astype(F32) * 0.1
    zx[64:72, :] = jnp.concatenate(
        [above[BZ : BZ + 1, :], jnp.zeros((6, C), F32), below[BZ : BZ + 1, :]], axis=0
    )
    for i in range(9):
        rows = slice(i * 8, i * 8 + 8)
        zw = pltpu.roll(fromw[8, rows, :], 19 - 8, 1)
        ze = pltpu.roll(frome[8, rows, :], 12 - 8, 1)
        zs[rows, :] = jnp.where(pos == 19, zw, jnp.where(pos == 12, ze, 0.0))

    in_w, in_e = (pos >= 16) & (pos < 20), (pos >= 12) & (pos < 16)
    in_w3, in_e3 = (pos >= 17) & (pos < 20), (pos >= 12) & (pos < 15)

    def strip_step(step, carry):
        lq2 = jnp.maximum(step - 2, 0)
        lq = jnp.minimum(step, LQ - 1)
        pk2 = 7 + lq2 // 8

        def emit(v, i, val):
            rows = slice(i * 8, i * 8 + 8)
            q = (lq2 % 8) * 4 + v
            fw = pltpu.roll(fromw[pk2, rows, :], (19 - q + C) % C, 1)
            fe = pltpu.roll(frome[pk2, rows, :], (12 - q + C) % C, 1)
            fs = jnp.where(pos == 19, fw, jnp.where(pos == 12, fe, 0.0))
            sr[lq2, v, rows, :] = val + zs[rows, :] * (fs - val)

        stage_three(f2, c2, w2, emit)
        stage_two(f1, c1, w1, f2, c2, w2)
        pk = lq // 2
        for v in range(V):
            q4 = ((lq % 2) * 4 + v) * 4
            for i in range(9):
                rows = slice(i * 8, i * 8 + 8)
                sw = pltpu.roll(fromw[pk, rows, :], (16 - q4 + C) % C, 1)
                se = pltpu.roll(frome[pk, rows, :], (12 - q4 + C) % C, 1)
                put_ring(x, v, i, jnp.where(in_w, sw, jnp.where(in_e, se, strips[lq, v, rows, :])))

        def wind_at(k, i):
            rows = slice(i * 8, i * 8 + 8)
            sw = pltpu.roll(fromw[5 + k, rows, :], (17 - lq * 3 + C) % C, 1)
            se = pltpu.roll(frome[5 + k, rows, :], (12 - lq * 3 + C) % C, 1)
            return jnp.where(in_w3, sw, jnp.where(in_e3, se, wstrips[lq, k, rows, :]))

        stage_one(x, wind_at, diff, f1, c1, w1)
        return carry

    lax.fori_loop(0, LQ + 2, strip_step, 0)

    lo, hi = lane <= 2, lane >= 125

    def merge_one(v, lq, j):
        level = lq * 4 + j
        f = v * L + level
        fmain = forcing[v, level].astype(F32)
        for i in range(9):
            rows = slice(i * 8, i * 8 + 8)
            s = sr[lq, v, rows, :]
            te = pltpu.roll(s, (127 - (j * 32 + 11)) % C, 1)
            tw = pltpu.roll(s, (-(j * 32 + 20)) % C, 1)
            t = jnp.where(lo, tw, jnp.where(hi, te, third[v, level, rows, :]))
            if i < 8:
                fv = fmain[i * 8 : i * 8 + 8]
            else:
                fv = jnp.concatenate(
                    [above[pl.ds(BF + f, 1), :], jnp.zeros((6, C), F32), below[pl.ds(BF + f, 1), :]], axis=0
                )
            r = t + zx[rows, :] * (fv - t)
            at = pl.ds((i * 8 + 1) * PITCH + f, 8, stride=PITCH)
            y0[at, :] = r
            ym[at, :] = pltpu.roll(jnp.where(lane == 127, tw, r), 1, 1)
            yp[at, :] = pltpu.roll(jnp.where(lane == 0, te, r), C - 1, 1)

    def merge(lq, carry):
        for v in range(V):
            for j in range(4):
                merge_one(v, lq, j)
        return carry

    lax.fori_loop(0, LQ - 1, merge, 0)
    for v in range(V):
        merge_one(v, LQ - 1, 0)

    def hot(yb, carry):
        lnd = land[pl.ds(yb * 8, 8), :]
        ter = terrain[pl.ds(yb * 8, 8), :]
        for k in range(8):
            j = iota((16, C), 0)
            oh = jnp.where(j < 2, jnp.where(j == lnd[k : k + 1], 1.0, 0.0), jnp.where(j - 2 == ter[k : k + 1], 1.0, 0.0))
            base = (yb * 8 + k + 1) * PITCH + F
            y0[pl.ds(base, 10), :] = oh[0:10]
            ym[pl.ds(base, 10), :] = jnp.zeros((10, C), F32)
            yp[pl.ds(base, 10), :] = jnp.zeros((10, C), F32)
        return carry

    lax.fori_loop(0, 8, hot, 0)
    for ref in (y0, ym, yp):
        for p in (65, 72):
            ref[p * PITCH + F : p * PITCH + F + 10, :] = jnp.zeros((10, C), F32)
        ref[73 * PITCH : 73 * PITCH + 8, :] = jnp.zeros((8, C), F32)
        ref[66 * PITCH : 66 * PITCH + 8, :] = jnp.zeros((8, C), F32)

    def convert(p, carry):
        src = jnp.where(p == 0, 72, p) * PITCH
        dst = pl.multiple_of(p * KP, 16)
        for a, b in ((y0, b0), (ym, bm), (yp, bp)):
            b[pl.ds(dst, KP), :] = a[pl.ds(src, KP), :].astype(BF16)
        return carry

    lax.fori_loop(0, 66, convert, 0)

    def network(t, carry):
        acc = jnp.zeros((256, 256), F32)
        for k, b in enumerate((bm, b0, bp)):
            pair = jnp.concatenate(
                [b[pl.ds(pl.multiple_of((2 * t + u) * KP, 16), 3 * KP), :] for u in range(2)], axis=1
            )
            acc = acc + jnp.dot(wb[k], pair, preferred_element_type=F32)
        a1 = silu(acc).astype(BF16)
        a2 = silu(jnp.dot(w2t[...], a1, preferred_element_type=F32)).astype(BF16)
        ph = jnp.dot(w3t[...], a2, preferred_element_type=F32)
        for u in range(2):
            at = pl.ds((2 * t + u + 1) * PITCH, F)
            y0[at, :] = y0[at, :] + ph[:F, u * C : u * C + C]
        return carry

    lax.fori_loop(0, R // 2, network, 0)

    def write(f, carry):
        for i in range(8):
            out[f, i * 8 : i * 8 + 8, :] = y0[pl.ds((i * 8 + 1) * PITCH + f, 8, stride=PITCH), :]
        return carry

    lax.fori_loop(0, F, write, 0, unroll=4)


def run_last(*args):
    n = 74 * PITCH
    scratch = stage_scratch() + [
        pltpu.VMEM((LQ, V, E, C), F32),
        pltpu.VMEM((E, C), F32),
        pltpu.VMEM((E, C), F32),
    ]
    scratch += [pltpu.VMEM((n, C), F32)] * 3 + [pltpu.VMEM((66 * KP, C), BF16)] * 3
    return pl.pallas_call(
        last,
        out_shape=jax.ShapeDtypeStruct((F, R, C), F32),
        in_specs=[pl.BlockSpec(memory_space=pltpu.VMEM)] * len(args),
        out_specs=pl.BlockSpec(memory_space=pltpu.VMEM),
        scratch_shapes=scratch,
        compiler_params=pltpu.CompilerParams(vmem_limit_bytes=LIM),
        cost_estimate=pl.CostEstimate(flops=9_000_000_000, bytes_accessed=20_000_000, transcendentals=4_000_000),
        name="strips_and_network",
    )(*args)


def local(state, wind, forcing, zone, land, terrain, first_weight, second_weight, third_weight, land_embed, terrain_embed):
    def shifts(axis):
        size = lax.axis_size(axis)
        up = [(i, i + 1) for i in range(size - 1)]
        return up, [(j, i) for i, j in up]

    down_buf, up_buf = pack_north_south(state, wind.reshape(2 * L, R, C), forcing, zone)
    up, down = shifts("gy")
    below = lax.ppermute(up_buf, "gy", up)
    above = lax.ppermute(down_buf, "gy", down)

    extra = jnp.concatenate([land_embed, terrain_embed, jnp.zeros((256, 2), BF16)], axis=1)
    zero = jnp.zeros((256, KP - F), BF16)
    wb = []
    for b in range(3):
        parts = []
        for a in range(3):
            parts += [first_weight[3 * a + b], extra if (a == 1 and b == 1) else zero]
        wb.append(jnp.concatenate(parts, axis=1))
    wb = jnp.stack(wb)
    w3 = jnp.concatenate([third_weight, jnp.zeros((KP - F, 256), BF16)], axis=0)

    shaped = state.reshape(V, L, R, C)
    forced = forcing.reshape(V, L, R, C)
    strips, wstrips, east, west = pack_east_west(shaped, wind, forced, zone, below, above)
    up, down = shifts("gx")
    fromw = lax.ppermute(east, "gx", up)
    frome = lax.ppermute(west, "gx", down)
    third = run_main(shaped, wind, below, above)
    return run_last(
        third, strips, wstrips, fromw, frome, forced, zone, land, terrain, below, above, wb, second_weight, w3
    )


def solution(mesh):
    in_specs = (
        P(None, "gy", "gx"),
        P(None, None, "gy", "gx"),
        P(None, "gy", "gx"),
        P("gy", "gx"),
        P("gy", "gx"),
        P("gy", "gx"),
        P(),
        P(),
        P(),
        P(),
        P(),
    )
    out_specs = P(None, "gy", "gx")
    return jax.shard_map(local, mesh=mesh, in_specs=in_specs, out_specs=out_specs, check_vma=False)
```

```python
import jax
import jax.numpy as jnp
from jax import lax
from jax.experimental import pallas as pl
from jax.experimental.pallas import tpu as pltpu
from jax.sharding import PartitionSpec as P

F32, BF16 = jnp.float32, jnp.bfloat16
V, L, F, R, C = 4, 37, 148, 64, 128
LQ = 10
E = 72
BW, BF, BZ, BN = 592, 888, 1036, 1048
PITCH = 158
KP = 160
LIM = 60 << 20
THIRD = 1.0 / 3.0


def iota(shape, dim):
    return lax.broadcasted_iota(jnp.int32, shape, dim)


def ns_pack(s0, s7, w0, w7, f0, f3, z0, z7, down, up):
    for f in range(F):
        down[f * 4 : f * 4 + 4, :] = s0[f, 0:4, :]
        up[f * 4 : f * 4 + 4, :] = s7[f, 4:8, :]
    for w in range(2 * L):
        down[BW + w * 4 : BW + w * 4 + 4, :] = w0[w, 0:4, :]
        up[BW + w * 4 : BW + w * 4 + 4, :] = w7[w, 4:8, :]
    for f in range(F):
        down[BF + f : BF + f + 1, :] = f0[f].astype(F32)[0:1]
        up[BF + f : BF + f + 1, :] = f3[f].astype(F32)[15:16]
    down[BZ : BZ + 8, :] = z0[...].astype(F32) * 0.1
    zu = z7[...].astype(F32) * 0.1
    up[BZ : BZ + 1, :] = zu[7:8]
    up[BZ + 1 : BN, :] = jnp.zeros((BN - BZ - 1, C), F32)
    down[BZ + 8 : BN, :] = jnp.zeros((BN - BZ - 8, C), F32)


def pack_north_south(state, wind, forcing, zone):
    st = jax.ShapeDtypeStruct((BN, C), F32)
    full = pl.BlockSpec((BN, C), lambda i: (0, 0))
    return pl.pallas_call(
        ns_pack,
        grid=(1,),
        out_shape=(st, st),
        in_specs=[
            pl.BlockSpec((F, 8, C), lambda i: (0, 0, 0)),
            pl.BlockSpec((F, 8, C), lambda i: (0, 7, 0)),
            pl.BlockSpec((2 * L, 8, C), lambda i: (0, 0, 0)),
            pl.BlockSpec((2 * L, 8, C), lambda i: (0, 7, 0)),
            pl.BlockSpec((F, 16, C), lambda i: (0, 0, 0)),
            pl.BlockSpec((F, 16, C), lambda i: (0, 3, 0)),
            pl.BlockSpec((8, C), lambda i: (0, 0)),
            pl.BlockSpec((8, C), lambda i: (7, 0)),
        ],
        out_specs=(full, full),
        compiler_params=pltpu.CompilerParams(vmem_limit_bytes=LIM),
        name="ns_pack",
    )(state, state, wind, wind, forcing, forcing, zone, zone)


def selector(j, ring):
    lane = iota((C, C), 1)
    col = iota((C, C), 0)
    pos = lane % 32
    if ring:
        want = jnp.where(pos == 11, 127, jnp.where(pos == 20, 0, -1))
    else:
        want = jnp.where(pos < 12, 116 + pos, jnp.where(pos >= 20, pos - 20, -1))
    return jnp.where((want == col) & (lane // 32 == j), 1.0, 0.0).astype(BF16)


def split(x):
    hi = x.astype(BF16)
    lo = (x - hi.astype(F32)).astype(BF16)
    return hi, lo


def fill_selectors(sel, rsel):
    for j in range(4):
        one = selector(j, False)
        sel[2 * j * C : (2 * j + 1) * C, :] = one
        sel[(2 * j + 1) * C : (2 * j + 2) * C, :] = one
        rsel[j * C : (j + 1) * C, :] = selector(j, True)


def stack(parts):
    return parts[0] if len(parts) == 1 else jnp.concatenate(parts, axis=0)


def strip_of(get, keys, sel):
    wide = []
    for j in range(4):
        wide += list(split(stack([get(key, j) for key in keys])))
    return jnp.dot(jnp.concatenate(wide, axis=1), sel[...], preferred_element_type=F32)


def ring_of(get, keys, rsel):
    wide = [stack([get(key, j) for key in keys]).astype(BF16) for j in range(4)]
    return jnp.dot(jnp.concatenate(wide, axis=1), rsel[...], preferred_element_type=F32)


def zone_lanes(zed, last_column):
    only = jnp.where(iota(zed.shape, 1) == 8, pltpu.roll(zed, 9 if last_column else 8, 1), 0.0)
    tot = only
    for j in range(1, 4):
        tot = tot + pltpu.roll(only, j * 32, 1)
    return tot


def put_strip(ref, p, q, width, s, start, rows):
    lane = iota((rows, C), 1) % 32
    inside = (lane >= q * width) & (lane < q * width + width)
    ref[p] = jnp.where(inside, pltpu.roll(s, (q * width - start + C) % C, 1), ref[p])


def ew_pack(state, wind, forcing, zone, strips, wstrips, east, west, sel, rsel):
    lg = pl.program_id(0)

    @pl.when(lg == 0)
    def _():
        fill_selectors(sel, rsel)
        zed = zone[...].astype(F32) * 0.1
        for ref, at_end in ((east, True), (west, False)):
            ref[...] = jnp.zeros((9, R, C), F32)
            ref[8] = zone_lanes(zed, at_end)

    def clean(x, i):
        return x if i < 5 else jnp.where(lg * 8 + i < L, x, 0.0)

    keys = [(m, v) for m in range(2) for v in range(V)]
    wkeys = [(m, c) for m in range(2) for c in range(2)]
    s = strip_of(lambda k, j: clean(state[k[1], k[0] * 4 + j], k[0] * 4 + j), keys, sel)
    f = ring_of(lambda k, j: clean(forcing[k[1], k[0] * 4 + j].astype(F32), k[0] * 4 + j), keys, rsel)
    w = strip_of(lambda k, j: clean(wind[k[1], k[0] * 4 + j], k[0] * 4 + j), wkeys, sel)
    pk = 7 + lg // 4
    for q, (m, v) in enumerate(keys):
        part = s[q * R : q * R + R]
        strips[m, v] = part
        put_strip(east, lg, q, 4, part, 8, R)
        put_strip(west, lg, q, 4, part, 20, R)
        part = f[q * R : q * R + R]
        qq = (lg % 4) * 8 + q
        put_strip(east, pk, qq, 1, part, 11, R)
        put_strip(west, pk, qq, 1, part, 20, R)
    for n, (m, c) in enumerate(wkeys):
        part = w[n * R : n * R + R]
        wstrips[m, c] = part
        put_strip(east, 5 + c, lg * 2 + m, 3, part, 9, R)
        put_strip(west, 5 + c, lg * 2 + m, 3, part, 20, R)


def ew_pack_halo(below, above, s_in, w_in, e_in, x_in, strips, wstrips, east, west, sel, rsel):
    fill_selectors(sel, rsel)
    zero = jnp.zeros((8, C), F32)

    def single(row):
        return jnp.concatenate([above[row : row + 1, :], zero[:6], below[row : row + 1, :]], axis=0)

    def four(row):
        return jnp.concatenate([above[row : row + 4, :], below[row : row + 4, :]], axis=0)

    def state_at(k, j):
        level = k[0] * 4 + j
        return four((k[1] * L + level) * 4) if level < L else zero

    def wind_at(k, j):
        level = k[0] * 4 + j
        return four(BW + (k[1] * L + level) * 4) if level < L else zero

    def force_at(k, j):
        level = k[0] * 4 + j
        return single(BF + k[1] * L + level) if level < L else zero

    keys = [(m, v) for m in range(LQ) for v in range(V)]
    wkeys = [(m, c) for m in range(LQ) for c in range(2)]
    s = strip_of(state_at, keys, sel)
    f = ring_of(force_at, keys, rsel)
    w = strip_of(wind_at, wkeys, sel)
    zed = single(BZ)
    for ref, at_end in ((east, True), (west, False)):
        ref[...] = jnp.zeros((9, 8, C), F32)
        ref[8] = zone_lanes(zed, at_end)
    for n, (m, v) in enumerate(keys):
        part = s[n * 8 : n * 8 + 8]
        strips[m, v] = part
        put_strip(east, n // 8, n % 8, 4, part, 8, 8)
        put_strip(west, n // 8, n % 8, 4, part, 20, 8)
        part = f[n * 8 : n * 8 + 8]
        put_strip(east, 7 + n // 32, n % 32, 1, part, 11, 8)
        put_strip(west, 7 + n // 32, n % 32, 1, part, 20, 8)
    for n, (m, c) in enumerate(wkeys):
        part = w[n * 8 : n * 8 + 8]
        wstrips[m, c] = part
        put_strip(east, 5 + c, m, 3, part, 9, 8)
        put_strip(west, 5 + c, m, 3, part, 20, 8)


SELECTORS = [pltpu.VMEM((8 * C, C), BF16), pltpu.VMEM((4 * C, C), BF16)]
PACKED = (
    jax.ShapeDtypeStruct((LQ, V, E, C), F32),
    jax.ShapeDtypeStruct((LQ, 2, E, C), F32),
    jax.ShapeDtypeStruct((9, E, C), F32),
    jax.ShapeDtypeStruct((9, E, C), F32),
)


def pack_east_west(state, wind, forcing, zone):
    return pl.pallas_call(
        ew_pack,
        grid=(5,),
        out_shape=PACKED,
        in_specs=[
            pl.BlockSpec((V, 8, R, C), lambda i: (0, i, 0, 0)),
            pl.BlockSpec((2, 8, R, C), lambda i: (0, i, 0, 0)),
            pl.BlockSpec((V, 8, R, C), lambda i: (0, i, 0, 0)),
            pl.BlockSpec((R, C), lambda i: (0, 0)),
        ],
        out_specs=(
            pl.BlockSpec((2, V, R, C), lambda i: (i, 0, 0, 0)),
            pl.BlockSpec((2, 2, R, C), lambda i: (i, 0, 0, 0)),
            pl.BlockSpec((9, R, C), lambda i: (0, 0, 0)),
            pl.BlockSpec((9, R, C), lambda i: (0, 0, 0)),
        ),
        scratch_shapes=SELECTORS,
        compiler_params=pltpu.CompilerParams(vmem_limit_bytes=LIM),
        cost_estimate=pl.CostEstimate(flops=4_000_000_000, bytes_accessed=13_000_000, transcendentals=0),
        name="ew_pack",
    )(state, wind, forcing, zone)


def pack_halo(below, above, packed):
    hbm = pl.BlockSpec(memory_space=pl.ANY)
    return pl.pallas_call(
        ew_pack_halo,
        grid=(1,),
        out_shape=PACKED,
        in_specs=[pl.BlockSpec((BN, C), lambda i: (0, 0))] * 2 + [hbm] * 4,
        out_specs=(
            pl.BlockSpec((LQ, V, 8, C), lambda i: (0, 0, 8, 0)),
            pl.BlockSpec((LQ, 2, 8, C), lambda i: (0, 0, 8, 0)),
            pl.BlockSpec((9, 8, C), lambda i: (0, 8, 0)),
            pl.BlockSpec((9, 8, C), lambda i: (0, 8, 0)),
        ),
        scratch_shapes=SELECTORS,
        input_output_aliases={2: 0, 3: 1, 4: 2, 5: 3},
        compiler_params=pltpu.CompilerParams(vmem_limit_bytes=LIM),
        name="ew_pack_halo",
    )(below, above, *packed)


def put_ring(ref, v, i, val):
    ref[v, 8 + i * 8 : 16 + i * 8, :] = val
    if i == 0:
        ref[v, 80:81, :] = val[0:1]
    if i == 8:
        ref[v, 7:8, :] = val[7:8]


def around(ref, v, i):
    q = ref[v, 8 + i * 8 : 16 + i * 8, :]
    n = ref[v, 9 + i * 8 : 17 + i * 8, :]
    s = ref[v, 7 + i * 8 : 15 + i * 8, :]
    return q, pltpu.roll(q, C - 1, 1), pltpu.roll(q, 1, 1), n, s


def stage_three(f2, c2, w2, emit):
    for i in range(9):
        rows = slice(i * 8, i * 8 + 8)
        ce, cw, cn, cs = (w2[k, rows, :] for k in range(4))
        for v in range(V):
            q, e, w, n, s = around(f2, v, i)
            g = (ce * e + cw * w) + (cn * n + cs * s)
            emit(v, i, THIRD * c2[v, rows, :] + (2.0 * THIRD) * (0.6 * q + g))


def stage_two(f1, c1, w1, f2, c2, w2):
    for i in range(9):
        rows = slice(i * 8, i * 8 + 8)
        ce, cw, cn, cs = (w1[k, rows, :] for k in range(4))
        for v in range(V):
            q, e, w, n, s = around(f1, v, i)
            g = (ce * e + cw * w) + (cn * n + cs * s)
            c = c1[v, rows, :]
            c2[v, rows, :] = c
            put_ring(f2, v, i, 0.75 * c + 0.25 * (0.6 * q + g))
        for k, val in enumerate((ce, cw, cn, cs)):
            w2[k, rows, :] = val


def stage_one(x, wind_at, diff, f1, c1, w1):
    for i in range(9):
        rows = slice(i * 8, i * 8 + 8)
        d = diff[rows, :]
        hu, hv = (0.5 * wind_at(k, i) for k in range(2))
        ce, cw, cn, cs = d - hu, d + hu, d - hv, d + hv
        for v in range(V):
            q, e, w, n, s = around(x, v, i)
            g = (ce * e + cw * w) + (cn * n + cs * s)
            c1[v, rows, :] = q
            put_ring(f1, v, i, 0.6 * q + g)
        for k, val in enumerate((ce, cw, cn, cs)):
            w1[k, rows, :] = val


def diffusion(strip):
    row, lane = iota((E, C), 0), iota((E, C), 1)
    gy, gx = lax.axis_index("gy"), lax.axis_index("gx")
    ok_above = jnp.where(gy < lax.axis_size("gy") - 1, 1, 0)
    ok_below = jnp.where(gy > 0, 1, 0)
    ok = jnp.where(row < 64, 1, jnp.where(row < 68, ok_above, ok_below))
    if strip:
        pos = lane % 32
        ok_east = jnp.where(gx < lax.axis_size("gx") - 1, 1, 0)
        ok_west = jnp.where(gx > 0, 1, 0)
        ok = ok * jnp.where((pos >= 12) & (pos < 16), ok_east, jnp.where((pos >= 16) & (pos < 20), ok_west, 1))
    return 0.1 * ok.astype(F32)


def stage_scratch():
    return [
        pltpu.VMEM((V, 88, C), F32),
        pltpu.VMEM((V, 88, C), F32),
        pltpu.VMEM((V, 88, C), F32),
        pltpu.VMEM((V, E, C), F32),
        pltpu.VMEM((V, E, C), F32),
        pltpu.VMEM((4, E, C), F32),
        pltpu.VMEM((4, E, C), F32),
        pltpu.VMEM((E, C), F32),
    ]


def main_stages(state, wind, below, above, third, x, f1, f2, c1, c2, w1, w2, diff):
    block = pl.program_id(0)

    @pl.when(block == 0)
    def _():
        diff[...] = diffusion(False)

    def one(k, carry):
        level = jnp.minimum(block * 8 + k, L - 1)

        def emit(v, i, val):
            third[v, k, i * 8 : i * 8 + 8, :] = val

        stage_three(f2, c2, w2, emit)
        stage_two(f1, c1, w1, f2, c2, w2)
        for v in range(V):
            for i in range(8):
                put_ring(x, v, i, state[v, k, i * 8 : i * 8 + 8, :])
            at = pl.ds((v * L + level) * 4, 4)
            put_ring(x, v, 8, jnp.concatenate([above[at, :], below[at, :]], axis=0))

        def wind_at(c, i):
            if i < 8:
                return wind[c, k, i * 8 : i * 8 + 8, :]
            at = pl.ds(BW + (c * L + level) * 4, 4)
            return jnp.concatenate([above[at, :], below[at, :]], axis=0)

        stage_one(x, wind_at, diff, f1, c1, w1)
        return carry

    lax.fori_loop(0, 8, one, 0)


def run_main(state, wind, below, above):
    return pl.pallas_call(
        main_stages,
        grid=(5,),
        out_shape=jax.ShapeDtypeStruct((V, 40, E, C), F32),
        in_specs=[
            pl.BlockSpec((V, 8, R, C), lambda i: (0, i, 0, 0)),
            pl.BlockSpec((2, 8, R, C), lambda i: (0, i, 0, 0)),
            pl.BlockSpec((BN, C), lambda i: (0, 0)),
            pl.BlockSpec((BN, C), lambda i: (0, 0)),
        ],
        out_specs=pl.BlockSpec((V, 8, E, C), lambda i: (0, i, 0, 0)),
        scratch_shapes=stage_scratch(),
        compiler_params=pltpu.CompilerParams(vmem_limit_bytes=LIM),
        cost_estimate=pl.CostEstimate(flops=60_000_000, bytes_accessed=13_000_000, transcendentals=0),
        name="main_stages",
    )(state, wind, below, above)


def silu(v):
    h = 0.5 * v
    return h + h * jnp.tanh(h)


def last(
    third_any, forcing_any, strips, wstrips, fromw, frome, zone, land, terrain, below, above, wb, w2t, w3t,
    out_any,
    x, f1, f2, c1, c2, w1, w2, diff, sr, zs, zx, y0, ym, yp, b0, bm, bp, third, forcing, h1, h2, out, sems,
):
    get_third = pltpu.make_async_copy(third_any, third, sems.at[0])
    get_forcing = pltpu.make_async_copy(forcing_any, forcing, sems.at[1])
    get_third.start()
    get_forcing.start()
    lane = iota((8, C), 1)
    pos = lane % 32
    diff[...] = diffusion(True)
    zx[0:64, :] = zone[...].astype(F32) * 0.1
    zx[64:72, :] = jnp.concatenate(
        [above[BZ : BZ + 1, :], jnp.zeros((6, C), F32), below[BZ : BZ + 1, :]], axis=0
    )
    for i in range(9):
        rows = slice(i * 8, i * 8 + 8)
        zw = pltpu.roll(fromw[8, rows, :], 19 - 8, 1)
        ze = pltpu.roll(frome[8, rows, :], 12 - 8, 1)
        zs[rows, :] = jnp.where(pos == 19, zw, jnp.where(pos == 12, ze, 0.0))

    in_w, in_e = (pos >= 16) & (pos < 20), (pos >= 12) & (pos < 16)
    in_w3, in_e3 = (pos >= 17) & (pos < 20), (pos >= 12) & (pos < 15)

    def strip_step(step, carry):
        lq2 = jnp.maximum(step - 2, 0)
        lq = jnp.minimum(step, LQ - 1)
        pk2 = 7 + lq2 // 8

        def emit(v, i, val):
            rows = slice(i * 8, i * 8 + 8)
            q = (lq2 % 8) * 4 + v
            fw = pltpu.roll(fromw[pk2, rows, :], (19 - q + C) % C, 1)
            fe = pltpu.roll(frome[pk2, rows, :], (12 - q + C) % C, 1)
            fs = jnp.where(pos == 19, fw, jnp.where(pos == 12, fe, 0.0))
            sr[lq2, v, rows, :] = val + zs[rows, :] * (fs - val)

        stage_three(f2, c2, w2, emit)
        stage_two(f1, c1, w1, f2, c2, w2)
        pk = lq // 2
        for v in range(V):
            q4 = ((lq % 2) * 4 + v) * 4
            for i in range(9):
                rows = slice(i * 8, i * 8 + 8)
                sw = pltpu.roll(fromw[pk, rows, :], (16 - q4 + C) % C, 1)
                se = pltpu.roll(frome[pk, rows, :], (12 - q4 + C) % C, 1)
                put_ring(x, v, i, jnp.where(in_w, sw, jnp.where(in_e, se, strips[lq, v, rows, :])))

        def wind_at(k, i):
            rows = slice(i * 8, i * 8 + 8)
            sw = pltpu.roll(fromw[5 + k, rows, :], (17 - lq * 3 + C) % C, 1)
            se = pltpu.roll(frome[5 + k, rows, :], (12 - lq * 3 + C) % C, 1)
            return jnp.where(in_w3, sw, jnp.where(in_e3, se, wstrips[lq, k, rows, :]))

        stage_one(x, wind_at, diff, f1, c1, w1)
        return carry

    lax.fori_loop(0, LQ + 2, strip_step, 0)

    get_third.wait()
    get_forcing.wait()
    lo, hi = lane <= 2, lane >= 125

    def merge_one(v, lq, j):
        level = lq * 4 + j
        f = v * L + level
        fmain = forcing[v, level].astype(F32)
        for i in range(9):
            rows = slice(i * 8, i * 8 + 8)
            s = sr[lq, v, rows, :]
            te = pltpu.roll(s, (127 - (j * 32 + 11)) % C, 1)
            tw = pltpu.roll(s, (-(j * 32 + 20)) % C, 1)
            t = jnp.where(lo, tw, jnp.where(hi, te, third[v, level + 2, rows, :]))
            if i < 8:
                fv = fmain[i * 8 : i * 8 + 8]
            else:
                fv = jnp.concatenate(
                    [above[pl.ds(BF + f, 1), :], jnp.zeros((6, C), F32), below[pl.ds(BF + f, 1), :]], axis=0
                )
            r = t + zx[rows, :] * (fv - t)
            at = pl.ds((i * 8 + 1) * PITCH + f, 8, stride=PITCH)
            y0[at, :] = r
            ym[at, :] = jnp.where(lane == 127, tw, r)
            yp[at, :] = jnp.where(lane == 0, te, r)

    def merge(lq, carry):
        for v in range(V):
            for j in range(4):
                merge_one(v, lq, j)
        return carry

    lax.fori_loop(0, LQ - 1, merge, 0)
    for v in range(V):
        merge_one(v, LQ - 1, 0)

    def hot(yb, carry):
        lnd = land[pl.ds(yb * 8, 8), :]
        ter = terrain[pl.ds(yb * 8, 8), :]
        for k in range(8):
            j = iota((16, C), 0)
            oh = jnp.where(j < 2, jnp.where(j == lnd[k : k + 1], 1.0, 0.0), jnp.where(j - 2 == ter[k : k + 1], 1.0, 0.0))
            base = (yb * 8 + k + 1) * PITCH + F
            y0[pl.ds(base, 10), :] = oh[0:10]
            ym[pl.ds(base, 10), :] = jnp.zeros((10, C), F32)
            yp[pl.ds(base, 10), :] = jnp.zeros((10, C), F32)
        return carry

    lax.fori_loop(0, 8, hot, 0)
    for ref in (y0, ym, yp):
        for p in (65, 72):
            ref[p * PITCH + F : p * PITCH + F + 10, :] = jnp.zeros((10, C), F32)
        ref[73 * PITCH : 73 * PITCH + 8, :] = jnp.zeros((8, C), F32)
        ref[66 * PITCH : 66 * PITCH + 8, :] = jnp.zeros((8, C), F32)

    def convert(p):
        src = jnp.where(p == 0, 72, p) * PITCH
        dst = pl.multiple_of(p * KP, 16)
        vals = [a[pl.ds(src, KP), :] for a in (ym, yp)]
        b0[pl.ds(dst, KP), :] = y0[pl.ds(src, KP), :].astype(BF16)
        bm[pl.ds(dst, KP), :] = pltpu.roll(vals[0], 1, 1).astype(BF16)
        bp[pl.ds(dst, KP), :] = pltpu.roll(vals[1], C - 1, 1).astype(BF16)

    for p in range(4):
        convert(p)

    def network(t, carry):
        a2 = silu(h2[...]).astype(BF16)
        a1 = silu(h1[...]).astype(BF16)
        tc = jnp.minimum(t, R // 2 - 1)
        acc = None
        for k, b in enumerate((bm, b0, bp)):
            pair = jnp.concatenate(
                [b[pl.ds(pl.multiple_of((2 * tc + u) * KP, 16), 3 * KP), :] for u in range(2)], axis=1
            )
            d = jnp.dot(wb[k], pair, preferred_element_type=F32)
            acc = d if acc is None else acc + d
        for u in range(2):
            convert(jnp.minimum(2 * t + 4 + u, 65))
        h1[...] = acc
        h2[...] = jnp.dot(w2t[...], a1, preferred_element_type=F32)
        ph = jnp.dot(w3t[...], a2, preferred_element_type=F32)
        base = jnp.where(t >= 2, 2 * t - 3, 66)
        for u in range(2):
            at = pl.ds((base + u) * PITCH, F)
            y0[at, :] = y0[at, :] + ph[:F, u * C : u * C + C]
        return carry

    def put(j, slot):
        rows = pl.ds(pl.multiple_of(j * 8, 8), 8)
        return pltpu.make_async_copy(out.at[slot], out_any.at[:, rows, :], sems.at[2 + slot])

    def write(j, carry):
        slot = j % 2

        @pl.when(j >= 2)
        def _():
            put(j - 2, slot).wait()

        for f in range(F):
            out[slot, f] = y0[pl.ds((j * 8 + 1) * PITCH + f, 8, stride=PITCH), :]
        put(j, slot).start()
        return carry

    def rows_of_eight(j, carry):
        lax.fori_loop(4 * j + 2, 4 * j + 6, network, 0)
        return write(j, carry)

    lax.fori_loop(0, 2, network, 0)
    lax.fori_loop(0, R // 8, rows_of_eight, 0)
    put(R // 8 - 2, 0).wait()
    put(R // 8 - 1, 1).wait()


def run_last(*args):
    n = 74 * PITCH
    scratch = stage_scratch() + [
        pltpu.VMEM((LQ, V, E, C), F32),
        pltpu.VMEM((E, C), F32),
        pltpu.VMEM((E, C), F32),
    ]
    scratch += [pltpu.VMEM((n, C), F32)] * 3 + [pltpu.VMEM((66 * KP, C), BF16)] * 3
    scratch += [
        pltpu.VMEM((V, 40, E, C), F32),
        pltpu.VMEM((V, L, R, C), BF16),
        pltpu.VMEM((256, 256), F32),
        pltpu.VMEM((256, 256), F32),
        pltpu.VMEM((2, F, 8, C), F32),
        pltpu.SemaphoreType.DMA((4,)),
    ]
    hbm = pl.BlockSpec(memory_space=pl.ANY)
    return pl.pallas_call(
        last,
        out_shape=jax.ShapeDtypeStruct((F, R, C), F32),
        in_specs=[hbm] * 2 + [pl.BlockSpec(memory_space=pltpu.VMEM)] * (len(args) - 2),
        out_specs=hbm,
        scratch_shapes=scratch,
        compiler_params=pltpu.CompilerParams(vmem_limit_bytes=LIM),
        cost_estimate=pl.CostEstimate(flops=9_000_000_000, bytes_accessed=20_000_000, transcendentals=4_000_000),
        name="strips_and_network",
    )(*args)


def local(state, wind, forcing, zone, land, terrain, first_weight, second_weight, third_weight, land_embed, terrain_embed):
    def shifts(axis):
        size = lax.axis_size(axis)
        up = [(i, i + 1) for i in range(size - 1)]
        return up, [(j, i) for i, j in up]

    down_buf, up_buf = pack_north_south(state, wind.reshape(2 * L, R, C), forcing, zone)
    up, down = shifts("gy")
    below = lax.ppermute(up_buf, "gy", up)
    above = lax.ppermute(down_buf, "gy", down)

    extra = jnp.concatenate([land_embed, terrain_embed, jnp.zeros((256, 2), BF16)], axis=1)
    zero = jnp.zeros((256, KP - F), BF16)
    wb = []
    for b in range(3):
        parts = []
        for a in range(3):
            parts += [first_weight[3 * a + b], extra if (a == 1 and b == 1) else zero]
        wb.append(jnp.concatenate(parts, axis=1))
    wb = jnp.stack(wb)
    w3 = jnp.concatenate([third_weight, jnp.zeros((KP - F, 256), BF16)], axis=0)

    shaped = state.reshape(V, L, R, C)
    forced = forcing.reshape(V, L, R, C)
    packed = pack_east_west(shaped, wind, forced, zone)
    strips, wstrips, east, west = pack_halo(below, above, packed)
    up, down = shifts("gx")
    fromw = lax.ppermute(east, "gx", up)
    frome = lax.ppermute(west, "gx", down)
    third = run_main(shaped, wind, below, above)
    return run_last(
        third, forced, strips, wstrips, fromw, frome, zone, land, terrain, below, above, wb, second_weight, w3
    )


def solution(mesh):
    in_specs = (
        P(None, "gy", "gx"),
        P(None, None, "gy", "gx"),
        P(None, "gy", "gx"),
        P("gy", "gx"),
        P("gy", "gx"),
        P("gy", "gx"),
        P(),
        P(),
        P(),
        P(),
        P(),
    )
    out_specs = P(None, "gy", "gx")
    return jax.shard_map(local, mesh=mesh, in_specs=in_specs, out_specs=out_specs, check_vma=False)
```

```python
import jax
import jax.numpy as jnp
from jax import lax
from jax.experimental import pallas as pl
from jax.experimental.pallas import tpu as pltpu
from jax.sharding import PartitionSpec as P

F32, BF16 = jnp.float32, jnp.bfloat16
V, L, F, R, C = 4, 37, 148, 64, 128
LQ = 10
E = 72
BW, BF, BZ, BN = 592, 888, 1036, 1048
PITCH = 158
KP = 160
THIRD = 1.0 / 3.0


def iota(shape, dim):
    return lax.broadcasted_iota(jnp.int32, shape, dim)


def ns_pack(s0, s7, w0, w7, f0, f3, z0, z7, down, up):
    for f in range(F):
        down[f * 4 : f * 4 + 4, :] = s0[f, 0:4, :]
        up[f * 4 : f * 4 + 4, :] = s7[f, 4:8, :]
    for w in range(2 * L):
        down[BW + w * 4 : BW + w * 4 + 4, :] = w0[w, 0:4, :]
        up[BW + w * 4 : BW + w * 4 + 4, :] = w7[w, 4:8, :]
    for f in range(F):
        down[BF + f : BF + f + 1, :] = f0[f].astype(F32)[0:1]
        up[BF + f : BF + f + 1, :] = f3[f].astype(F32)[15:16]
    down[BZ : BZ + 8, :] = z0[...].astype(F32) * 0.1
    zu = z7[...].astype(F32) * 0.1
    up[BZ : BZ + 1, :] = zu[7:8]
    up[BZ + 1 : BN, :] = jnp.zeros((BN - BZ - 1, C), F32)
    down[BZ + 8 : BN, :] = jnp.zeros((BN - BZ - 8, C), F32)


def pack_north_south(state, wind, forcing, zone):
    st = jax.ShapeDtypeStruct((BN, C), F32)
    full = pl.BlockSpec((BN, C), lambda i: (0, 0))
    return pl.pallas_call(
        ns_pack,
        grid=(1,),
        out_shape=(st, st),
        in_specs=[
            pl.BlockSpec((F, 8, C), lambda i: (0, 0, 0)),
            pl.BlockSpec((F, 8, C), lambda i: (0, 7, 0)),
            pl.BlockSpec((2 * L, 8, C), lambda i: (0, 0, 0)),
            pl.BlockSpec((2 * L, 8, C), lambda i: (0, 7, 0)),
            pl.BlockSpec((F, 16, C), lambda i: (0, 0, 0)),
            pl.BlockSpec((F, 16, C), lambda i: (0, 3, 0)),
            pl.BlockSpec((8, C), lambda i: (0, 0)),
            pl.BlockSpec((8, C), lambda i: (7, 0)),
        ],
        out_specs=(full, full),
        compiler_params=pltpu.CompilerParams(vmem_limit_bytes=24 << 20),
        name="ns_pack",
    )(state, state, wind, wind, forcing, forcing, zone, zone)


def selector(j, ring):
    lane = iota((C, C), 1)
    col = iota((C, C), 0)
    pos = lane % 32
    if ring:
        want = jnp.where(pos == 11, 127, jnp.where(pos == 20, 0, -1))
    else:
        want = jnp.where(pos < 12, 116 + pos, jnp.where(pos >= 20, pos - 20, -1))
    return jnp.where((want == col) & (lane // 32 == j), 1.0, 0.0).astype(BF16)


def split(x):
    hi = x.astype(BF16)
    lo = (x - hi.astype(F32)).astype(BF16)
    return hi, lo


def fill_selectors(sel, rsel):
    for j in range(4):
        one = selector(j, False)
        sel[2 * j * C : (2 * j + 1) * C, :] = one
        sel[(2 * j + 1) * C : (2 * j + 2) * C, :] = one
        rsel[j * C : (j + 1) * C, :] = selector(j, True)


def fetch(srcs, dsts, sems, first=0):
    copies = [pltpu.make_async_copy(a, b, sems.at[first + i]) for i, (a, b) in enumerate(zip(srcs, dsts))]
    for c in copies:
        c.start()
    return copies


def done(copies):
    for c in copies:
        c.wait()


def stack(parts):
    return parts[0] if len(parts) == 1 else jnp.concatenate(parts, axis=0)


def strip_of(get, keys, sel):
    wide = []
    for j in range(4):
        wide += list(split(stack([get(key, j) for key in keys])))
    return jnp.dot(jnp.concatenate(wide, axis=1), sel[...], preferred_element_type=F32)


def ring_of(get, keys, rsel):
    wide = [stack([get(key, j) for key in keys]).astype(BF16) for j in range(4)]
    return jnp.dot(jnp.concatenate(wide, axis=1), rsel[...], preferred_element_type=F32)


def zone_lanes(zed, last_column):
    only = jnp.where(iota(zed.shape, 1) == 8, pltpu.roll(zed, 9 if last_column else 8, 1), 0.0)
    tot = only
    for j in range(1, 4):
        tot = tot + pltpu.roll(only, j * 32, 1)
    return tot


def put_strips(old, width, start, parts):
    lane = iota(parts[0][1].shape, 1) % 32
    for q, s in parts:
        inside = (lane >= q * width) & (lane < q * width + width)
        old = jnp.where(inside, pltpu.roll(s, (q * width - start + C) % C, 1), old)
    return old


def prepare(first_t, land_t, terrain_t, wb):
    zero = jnp.zeros((KP - F, 256), F32)
    extra = jnp.concatenate([land_t[...].astype(F32), terrain_t[...].astype(F32), zero[:2]], axis=0)
    for b in range(3):
        tall = []
        for a in range(3):
            tall += [first_t[3 * a + b].astype(F32), extra if (a == 1 and b == 1) else zero]
        wb[b] = jnp.concatenate(tall, axis=0).T.astype(BF16)


def ew_pack(state, wind, forcing, zone, first_t, land_t, terrain_t, strips, wstrips, east, west, wb, sel, rsel):
    lg = pl.program_id(0)

    @pl.when(lg == 0)
    def _():
        fill_selectors(sel, rsel)
        zed = zone[...].astype(F32) * 0.1
        for ref, at_end in ((east, True), (west, False)):
            ref[...] = jnp.zeros((9, R, C), F32)
            ref[8] = zone_lanes(zed, at_end)
        prepare(first_t, land_t, terrain_t, wb)

    def clean(x, i):
        return x if i < 5 else jnp.where(lg * 8 + i < L, x, 0.0)

    keys = [(m, v) for m in range(2) for v in range(V)]
    wkeys = [(m, c) for m in range(2) for c in range(2)]
    s = strip_of(lambda k, j: clean(state[k[1], k[0] * 4 + j], k[0] * 4 + j), keys, sel)
    f = ring_of(lambda k, j: clean(forcing[k[1], k[0] * 4 + j].astype(F32), k[0] * 4 + j), keys, rsel)
    w = strip_of(lambda k, j: clean(wind[k[1], k[0] * 4 + j], k[0] * 4 + j), wkeys, sel)
    pk = 7 + lg // 4
    for q, (m, v) in enumerate(keys):
        strips[m, v] = s[q * R : q * R + R]
    for n, (m, c) in enumerate(wkeys):
        wstrips[m, c] = w[n * R : n * R + R]
    for i in range(8):
        rows = slice(i * 8, i * 8 + 8)

        def cut(val, n):
            return val[n * R + i * 8 : n * R + i * 8 + 8]

        for ref, at4, at1, at3 in ((east, 8, 11, 9), (west, 20, 20, 20)):
            ref[lg, rows, :] = put_strips(jnp.zeros((8, C), F32), 4, at4, [(q, cut(s, q)) for q in range(8)])
            ref[pk, rows, :] = put_strips(ref[pk, rows, :], 1, at1, [((lg % 4) * 8 + q, cut(f, q)) for q in range(8)])
            for c in range(2):
                ref[5 + c, rows, :] = put_strips(
                    ref[5 + c, rows, :], 3, at3, [(lg * 2 + m, cut(w, m * 2 + c)) for m in range(2)]
                )


def ew_pack_halo(below_any, above_any, s_in, w_in, e_in, x_in, strips, wstrips, east, west, sel, rsel, below, above, sems):
    get = fetch((below_any, above_any), (below, above), sems)
    fill_selectors(sel, rsel)
    done(get)
    zero = jnp.zeros((8, C), F32)

    def single(row):
        return jnp.concatenate([above[row : row + 1, :], zero[:6], below[row : row + 1, :]], axis=0)

    def four(row):
        return jnp.concatenate([above[row : row + 4, :], below[row : row + 4, :]], axis=0)

    def state_at(k, j):
        level = k[0] * 4 + j
        return four((k[1] * L + level) * 4) if level < L else zero

    def wind_at(k, j):
        level = k[0] * 4 + j
        return four(BW + (k[1] * L + level) * 4) if level < L else zero

    def force_at(k, j):
        level = k[0] * 4 + j
        return single(BF + k[1] * L + level) if level < L else zero

    keys = [(m, v) for m in range(LQ) for v in range(V)]
    wkeys = [(m, c) for m in range(LQ) for c in range(2)]
    s = strip_of(state_at, keys, sel)
    f = ring_of(force_at, keys, rsel)
    w = strip_of(wind_at, wkeys, sel)
    zed = single(BZ)

    def cut(val, n):
        return val[n * 8 : n * 8 + 8]

    for n, (m, v) in enumerate(keys):
        strips[m, v] = cut(s, n)
    for n, (m, c) in enumerate(wkeys):
        wstrips[m, c] = cut(w, n)
    for ref, at_end, at4, at1, at3 in ((east, True, 8, 11, 9), (west, False, 20, 20, 20)):
        for p in range(5):
            ref[p] = put_strips(zero, 4, at4, [(q, cut(s, p * 8 + q)) for q in range(8)])
        for c in range(2):
            ref[5 + c] = put_strips(zero, 3, at3, [(m, cut(w, m * 2 + c)) for m in range(LQ)])
        ref[7] = put_strips(zero, 1, at1, [(q, cut(f, q)) for q in range(32)])
        ref[8] = put_strips(zone_lanes(zed, at_end), 1, at1, [(q, cut(f, 32 + q)) for q in range(8)])


NS_SCRATCH = [pltpu.VMEM((BN, C), F32), pltpu.VMEM((BN, C), F32), pltpu.SemaphoreType.DMA((2,))]
SELECTORS = [pltpu.VMEM((8 * C, C), BF16), pltpu.VMEM((4 * C, C), BF16)]
PACKED = (
    jax.ShapeDtypeStruct((LQ, V, E, C), F32),
    jax.ShapeDtypeStruct((LQ, 2, E, C), F32),
    jax.ShapeDtypeStruct((9, E, C), F32),
    jax.ShapeDtypeStruct((9, E, C), F32),
)


def pack_east_west(state, wind, forcing, zone, first_t, land_t, terrain_t):
    return pl.pallas_call(
        ew_pack,
        grid=(5,),
        out_shape=PACKED + (jax.ShapeDtypeStruct((3, 256, 3 * KP), BF16),),
        in_specs=[
            pl.BlockSpec((V, 8, R, C), lambda i: (0, i, 0, 0)),
            pl.BlockSpec((2, 8, R, C), lambda i: (0, i, 0, 0)),
            pl.BlockSpec((V, 8, R, C), lambda i: (0, i, 0, 0)),
            pl.BlockSpec((R, C), lambda i: (0, 0)),
            pl.BlockSpec(first_t.shape, lambda i: (0, 0, 0)),
            pl.BlockSpec(land_t.shape, lambda i: (0, 0)),
            pl.BlockSpec(terrain_t.shape, lambda i: (0, 0)),
        ],
        out_specs=(
            pl.BlockSpec((2, V, R, C), lambda i: (i, 0, 0, 0)),
            pl.BlockSpec((2, 2, R, C), lambda i: (i, 0, 0, 0)),
            pl.BlockSpec((9, R, C), lambda i: (0, 0, 0)),
            pl.BlockSpec((9, R, C), lambda i: (0, 0, 0)),
            pl.BlockSpec((3, 256, 3 * KP), lambda i: (0, 0, 0)),
        ),
        scratch_shapes=SELECTORS,
        compiler_params=pltpu.CompilerParams(vmem_limit_bytes=32 << 20),
        cost_estimate=pl.CostEstimate(flops=4_000_000_000, bytes_accessed=13_000_000, transcendentals=0),
        name="ew_pack",
    )(state, wind, forcing, zone, first_t, land_t, terrain_t)


def pack_halo(below, above, packed):
    hbm = pl.BlockSpec(memory_space=pl.ANY)
    return pl.pallas_call(
        ew_pack_halo,
        grid=(1,),
        out_shape=PACKED,
        in_specs=[hbm] * 6,
        out_specs=(
            pl.BlockSpec((LQ, V, 8, C), lambda i: (0, 0, 8, 0)),
            pl.BlockSpec((LQ, 2, 8, C), lambda i: (0, 0, 8, 0)),
            pl.BlockSpec((9, 8, C), lambda i: (0, 8, 0)),
            pl.BlockSpec((9, 8, C), lambda i: (0, 8, 0)),
        ),
        scratch_shapes=SELECTORS + NS_SCRATCH,
        input_output_aliases={2: 0, 3: 1, 4: 2, 5: 3},
        compiler_params=pltpu.CompilerParams(vmem_limit_bytes=24 << 20),
        name="ew_pack_halo",
    )(below, above, *packed)


def put_ring(ref, v, i, val):
    ref[v, i * 8 : i * 8 + 8, :] = val


class Around:
    def __init__(self, ref):
        self.ref, self.have = ref, {}
        row = iota((8, C), 0)
        self.top, self.bottom = row == 7, row == 0

    def block(self, v, i):
        i = i % 9 + (9 if i == 9 else 0)
        if (v, i) not in self.have:
            k = i % 9
            q = self.ref[v, k * 8 : k * 8 + 8, :]
            self.have[v, i] = (q, pltpu.roll(q, 7, 0), pltpu.roll(q, 1, 0))
        return self.have[v, i]

    def __call__(self, v, i):
        if i == 0:
            q8 = self.ref[v, 64:72, :]
            before = pltpu.roll(q8, 1, 0)
        else:
            before = self.block(v, i - 1)[2]
        q, up, dn = self.block(v, i)
        n = jnp.where(self.top, self.block(v, i + 1)[1], up)
        s = jnp.where(self.bottom, before, dn)
        return q, pltpu.roll(q, C - 1, 1), pltpu.roll(q, 1, 1), n, s


def stage_three(f2, c2, w2, emit):
    at = Around(f2)
    for i in range(9):
        rows = slice(i * 8, i * 8 + 8)
        ce, cw, cn, cs = (w2[k, rows, :] for k in range(4))
        for v in range(V):
            q, e, w, n, s = at(v, i)
            g = (ce * e + cw * w) + (cn * n + cs * s)
            emit(v, i, THIRD * c2[v, rows, :] + (2.0 * THIRD) * (0.6 * q + g))


def stage_two(f1, c1, w1, f2, c2, w2):
    at = Around(f1)
    for i in range(9):
        rows = slice(i * 8, i * 8 + 8)
        ce, cw, cn, cs = (w1[k, rows, :] for k in range(4))
        for v in range(V):
            q, e, w, n, s = at(v, i)
            g = (ce * e + cw * w) + (cn * n + cs * s)
            c = c1[v, rows, :]
            c2[v, rows, :] = c
            put_ring(f2, v, i, 0.75 * c + 0.25 * (0.6 * q + g))
        for k, val in enumerate((ce, cw, cn, cs)):
            w2[k, rows, :] = val


def stage_one(x, wind_at, diff, f1, c1, w1):
    at = Around(x)
    for i in range(9):
        rows = slice(i * 8, i * 8 + 8)
        d = diff[rows, :]
        hu, hv = (0.5 * wind_at(k, i) for k in range(2))
        ce, cw, cn, cs = d - hu, d + hu, d - hv, d + hv
        for v in range(V):
            q, e, w, n, s = at(v, i)
            g = (ce * e + cw * w) + (cn * n + cs * s)
            c1[v, rows, :] = q
            put_ring(f1, v, i, 0.6 * q + g)
        for k, val in enumerate((ce, cw, cn, cs)):
            w1[k, rows, :] = val


def diffusion(strip):
    row, lane = iota((E, C), 0), iota((E, C), 1)
    gy, gx = lax.axis_index("gy"), lax.axis_index("gx")
    ok_above = jnp.where(gy < lax.axis_size("gy") - 1, 1, 0)
    ok_below = jnp.where(gy > 0, 1, 0)
    ok = jnp.where(row < 64, 1, jnp.where(row < 68, ok_above, ok_below))
    if strip:
        pos = lane % 32
        ok_east = jnp.where(gx < lax.axis_size("gx") - 1, 1, 0)
        ok_west = jnp.where(gx > 0, 1, 0)
        ok = ok * jnp.where((pos >= 12) & (pos < 16), ok_east, jnp.where((pos >= 16) & (pos < 20), ok_west, 1))
    return 0.1 * ok.astype(F32)


def stage_scratch():
    return [
        pltpu.VMEM((V, E, C), F32),
        pltpu.VMEM((V, E, C), F32),
        pltpu.VMEM((V, E, C), F32),
        pltpu.VMEM((V, E, C), F32),
        pltpu.VMEM((V, E, C), F32),
        pltpu.VMEM((4, E, C), F32),
        pltpu.VMEM((4, E, C), F32),
        pltpu.VMEM((E, C), F32),
    ]


def main_stages(state, wind, below, above, third, x, f1, f2, c1, c2, w1, w2, diff):
    block = pl.program_id(0)

    @pl.when(block == 0)
    def _():
        diff[...] = diffusion(False)

    def one(k, carry):
        level = jnp.minimum(block * 8 + k, L - 1)

        def emit(v, i, val):
            third[v, k, i * 8 : i * 8 + 8, :] = val

        stage_three(f2, c2, w2, emit)
        stage_two(f1, c1, w1, f2, c2, w2)
        for v in range(V):
            for i in range(8):
                put_ring(x, v, i, state[v, k, i * 8 : i * 8 + 8, :])
            at = pl.ds((v * L + level) * 4, 4)
            put_ring(x, v, 8, jnp.concatenate([above[at, :], below[at, :]], axis=0))

        def wind_at(c, i):
            if i < 8:
                return wind[c, k, i * 8 : i * 8 + 8, :]
            at = pl.ds(BW + (c * L + level) * 4, 4)
            return jnp.concatenate([above[at, :], below[at, :]], axis=0)

        stage_one(x, wind_at, diff, f1, c1, w1)
        return carry

    lax.fori_loop(0, 8, one, 0, unroll=4)


def run_main(state, wind, below, above):
    return pl.pallas_call(
        main_stages,
        grid=(5,),
        out_shape=jax.ShapeDtypeStruct((V, 40, E, C), F32),
        in_specs=[
            pl.BlockSpec((V, 8, R, C), lambda i: (0, i, 0, 0)),
            pl.BlockSpec((2, 8, R, C), lambda i: (0, i, 0, 0)),
            pl.BlockSpec((BN, C), lambda i: (0, 0)),
            pl.BlockSpec((BN, C), lambda i: (0, 0)),
        ],
        out_specs=pl.BlockSpec((V, 8, E, C), lambda i: (0, i, 0, 0)),
        scratch_shapes=stage_scratch(),
        compiler_params=pltpu.CompilerParams(vmem_limit_bytes=24 << 20),
        cost_estimate=pl.CostEstimate(flops=60_000_000, bytes_accessed=13_000_000, transcendentals=0),
        name="main_stages",
    )(state, wind, below, above)


def silu(v):
    h = 0.5 * v
    return h + h * jnp.tanh(h)


def last(*refs):
    ins, out_any, bufs = refs[:14], refs[14], refs[15:29]
    (x, f1, f2, c1, c2, w1, w2, diff, sr, zs, zx, y0, ym, yp, b0, bm, bp, h1, h2, out, sems) = refs[29:]
    (strips, wstrips, fromw, frome, zone, below, above, third, forcing, land, terrain, wb, w2t, w3t) = bufs
    get_edges = fetch(ins[:7], bufs[:7], sems)
    get_main = fetch(ins[7:11], bufs[7:11], sems, 7)
    get_weights = fetch(ins[11:], bufs[11:], sems, 11)
    done(get_edges)
    lane = iota((8, C), 1)
    pos = lane % 32
    diff[...] = diffusion(True)
    zx[0:64, :] = zone[...].astype(F32) * 0.1
    zx[64:72, :] = jnp.concatenate(
        [above[BZ : BZ + 1, :], jnp.zeros((6, C), F32), below[BZ : BZ + 1, :]], axis=0
    )
    for i in range(9):
        rows = slice(i * 8, i * 8 + 8)
        zw = pltpu.roll(fromw[8, rows, :], 19 - 8, 1)
        ze = pltpu.roll(frome[8, rows, :], 12 - 8, 1)
        zs[rows, :] = jnp.where(pos == 19, zw, jnp.where(pos == 12, ze, 0.0))

    in_w, in_e = (pos >= 16) & (pos < 20), (pos >= 12) & (pos < 16)
    in_w3, in_e3 = (pos >= 17) & (pos < 20), (pos >= 12) & (pos < 15)

    def strip_step(step, carry):
        lq2 = jnp.maximum(step - 2, 0)
        lq = jnp.minimum(step, LQ - 1)
        pk2 = 7 + lq2 // 8

        def emit(v, i, val):
            rows = slice(i * 8, i * 8 + 8)
            q = (lq2 % 8) * 4 + v
            fw = pltpu.roll(fromw[pk2, rows, :], (19 - q + C) % C, 1)
            fe = pltpu.roll(frome[pk2, rows, :], (12 - q + C) % C, 1)
            fs = jnp.where(pos == 19, fw, jnp.where(pos == 12, fe, 0.0))
            sr[lq2, v, rows, :] = val + zs[rows, :] * (fs - val)

        stage_three(f2, c2, w2, emit)
        stage_two(f1, c1, w1, f2, c2, w2)
        pk = lq // 2
        for v in range(V):
            q4 = ((lq % 2) * 4 + v) * 4
            for i in range(9):
                rows = slice(i * 8, i * 8 + 8)
                sw = pltpu.roll(fromw[pk, rows, :], (16 - q4 + C) % C, 1)
                se = pltpu.roll(frome[pk, rows, :], (12 - q4 + C) % C, 1)
                put_ring(x, v, i, jnp.where(in_w, sw, jnp.where(in_e, se, strips[lq, v, rows, :])))

        def wind_at(k, i):
            rows = slice(i * 8, i * 8 + 8)
            sw = pltpu.roll(fromw[5 + k, rows, :], (17 - lq * 3 + C) % C, 1)
            se = pltpu.roll(frome[5 + k, rows, :], (12 - lq * 3 + C) % C, 1)
            return jnp.where(in_w3, sw, jnp.where(in_e3, se, wstrips[lq, k, rows, :]))

        stage_one(x, wind_at, diff, f1, c1, w1)
        return carry

    lax.fori_loop(0, LQ + 2, strip_step, 0)

    done(get_main)
    lo, hi = lane <= 2, lane >= 125

    def merge_one(v, lq, j):
        level = lq * 4 + j
        f = v * L + level
        fmain = forcing[v, level].astype(F32)
        for i in range(9):
            rows = slice(i * 8, i * 8 + 8)
            s = sr[lq, v, rows, :]
            te = pltpu.roll(s, (127 - (j * 32 + 11)) % C, 1)
            tw = pltpu.roll(s, (-(j * 32 + 20)) % C, 1)
            t = jnp.where(lo, tw, jnp.where(hi, te, third[v, level + 2, rows, :]))
            if i < 8:
                fv = fmain[i * 8 : i * 8 + 8]
            else:
                fv = jnp.concatenate(
                    [above[pl.ds(BF + f, 1), :], jnp.zeros((6, C), F32), below[pl.ds(BF + f, 1), :]], axis=0
                )
            r = t + zx[rows, :] * (fv - t)
            at = pl.ds((i * 8 + 1) * PITCH + f, 8, stride=PITCH)
            y0[at, :] = r
            ym[at, :] = jnp.where(lane == 127, tw, r)
            yp[at, :] = jnp.where(lane == 0, te, r)

    def merge(lq, carry):
        for v in range(V):
            for j in range(4):
                merge_one(v, lq, j)
        return carry

    lax.fori_loop(0, LQ - 1, merge, 0)
    for v in range(V):
        merge_one(v, LQ - 1, 0)

    def hot(yb, carry):
        lnd = land[pl.ds(yb * 8, 8), :]
        ter = terrain[pl.ds(yb * 8, 8), :]
        for k in range(8):
            j = iota((16, C), 0)
            oh = jnp.where(j < 2, jnp.where(j == lnd[k : k + 1], 1.0, 0.0), jnp.where(j - 2 == ter[k : k + 1], 1.0, 0.0))
            base = (yb * 8 + k + 1) * PITCH + F
            y0[pl.ds(base, 10), :] = oh[0:10]
            ym[pl.ds(base, 10), :] = jnp.zeros((10, C), F32)
            yp[pl.ds(base, 10), :] = jnp.zeros((10, C), F32)
        return carry

    lax.fori_loop(0, 8, hot, 0)
    for ref in (y0, ym, yp):
        for p in (65, 72):
            ref[p * PITCH + F : p * PITCH + F + 10, :] = jnp.zeros((10, C), F32)
        ref[73 * PITCH : 73 * PITCH + 8, :] = jnp.zeros((8, C), F32)
        ref[66 * PITCH : 66 * PITCH + 8, :] = jnp.zeros((8, C), F32)

    def convert(p):
        src = jnp.where(p == 0, 72, p) * PITCH
        dst = pl.multiple_of(p * KP, 16)
        vals = [a[pl.ds(src, KP), :] for a in (ym, yp)]
        b0[pl.ds(dst, KP), :] = y0[pl.ds(src, KP), :].astype(BF16)
        bm[pl.ds(dst, KP), :] = pltpu.roll(vals[0], 1, 1).astype(BF16)
        bp[pl.ds(dst, KP), :] = pltpu.roll(vals[1], C - 1, 1).astype(BF16)

    for p in range(4):
        convert(p)
    done(get_weights)

    def network(t, carry):
        a2 = silu(h2[...]).astype(BF16)
        a1 = silu(h1[...]).astype(BF16)
        tc = jnp.minimum(t, R // 2 - 1)
        acc = None
        for k, b in enumerate((bm, b0, bp)):
            pair = jnp.concatenate(
                [b[pl.ds(pl.multiple_of((2 * tc + u) * KP, 16), 3 * KP), :] for u in range(2)], axis=1
            )
            d = jnp.dot(wb[k], pair, preferred_element_type=F32)
            acc = d if acc is None else acc + d
        for u in range(2):
            convert(jnp.minimum(2 * t + 4 + u, 65))
        h1[...] = acc
        h2[...] = jnp.dot(w2t[...], a1, preferred_element_type=F32)
        ph = jnp.dot(w3t[...], a2, preferred_element_type=F32)
        base = jnp.where(t >= 2, 2 * t - 3, 66)
        for u in range(2):
            at = pl.ds((base + u) * PITCH, F)
            y0[at, :] = y0[at, :] + ph[:F, u * C : u * C + C]
        return carry

    def put(j, slot):
        rows = pl.ds(pl.multiple_of(j * 8, 8), 8)
        return pltpu.make_async_copy(out.at[slot], out_any.at[:, rows, :], sems.at[14 + slot])

    def write(j, carry):
        slot = j % 2

        @pl.when(j >= 2)
        def _():
            put(j - 2, slot).wait()

        for f in range(F):
            out[slot, f] = y0[pl.ds((j * 8 + 1) * PITCH + f, 8, stride=PITCH), :]
        put(j, slot).start()
        return carry

    def rows_of_eight(j, carry):
        lax.fori_loop(0, 4, lambda i, c: network(4 * j + 2 + i, c), 0, unroll=4)
        return write(j, carry)

    lax.fori_loop(0, 2, network, 0)
    lax.fori_loop(0, R // 8, rows_of_eight, 0)
    put(R // 8 - 2, 0).wait()
    put(R // 8 - 1, 1).wait()


def run_last(*args):
    n = 74 * PITCH
    hbm = pl.BlockSpec(memory_space=pl.ANY)
    scratch = [pltpu.VMEM(a.shape, a.dtype) for a in args] + stage_scratch()
    scratch += [
        pltpu.VMEM((LQ, V, E, C), F32),
        pltpu.VMEM((E, C), F32),
        pltpu.VMEM((E, C), F32),
    ]
    scratch += [pltpu.VMEM((n, C), F32)] * 3 + [pltpu.VMEM((66 * KP, C), BF16)] * 3
    scratch += [
        pltpu.VMEM((256, 256), F32),
        pltpu.VMEM((256, 256), F32),
        pltpu.VMEM((2, F, 8, C), F32),
        pltpu.SemaphoreType.DMA((16,)),
    ]
    return pl.pallas_call(
        last,
        out_shape=jax.ShapeDtypeStruct((F, R, C), F32),
        in_specs=[hbm] * len(args),
        out_specs=hbm,
        scratch_shapes=scratch,
        compiler_params=pltpu.CompilerParams(vmem_limit_bytes=44 << 20),
        cost_estimate=pl.CostEstimate(flops=9_000_000_000, bytes_accessed=20_000_000, transcendentals=4_000_000),
        name="strips_and_network",
    )(*args)


def local(state, wind, forcing, zone, land, terrain, first_weight, second_weight, third_weight, land_embed, terrain_embed):
    def shifts(axis):
        size = lax.axis_size(axis)
        up = [(i, i + 1) for i in range(size - 1)]
        return up, [(j, i) for i, j in up]

    down_buf, up_buf = pack_north_south(state, wind.reshape(2 * L, R, C), forcing, zone)
    up, down = shifts("gy")
    below = lax.ppermute(up_buf, "gy", up)
    above = lax.ppermute(down_buf, "gy", down)

    shaped = state.reshape(V, L, R, C)
    forced = forcing.reshape(V, L, R, C)
    packed = pack_east_west(shaped, wind, forced, zone, first_weight.transpose(0, 2, 1), land_embed.T, terrain_embed.T)
    wb = packed[4]
    strips, wstrips, east, west = pack_halo(below, above, packed[:4])
    up, down = shifts("gx")
    fromw = lax.ppermute(east, "gx", up)
    frome = lax.ppermute(west, "gx", down)
    third = run_main(shaped, wind, below, above)
    return run_last(
        strips, wstrips, fromw, frome, zone, below, above, third, forced, land, terrain, wb, second_weight, third_weight
    )


def solution(mesh):
    in_specs = (
        P(None, "gy", "gx"),
        P(None, None, "gy", "gx"),
        P(None, "gy", "gx"),
        P("gy", "gx"),
        P("gy", "gx"),
        P("gy", "gx"),
        P(),
        P(),
        P(),
        P(),
        P(),
    )
    out_specs = P(None, "gy", "gx")
    return jax.shard_map(local, mesh=mesh, in_specs=in_specs, out_specs=out_specs, check_vma=False)
```

```python
import jax
import jax.numpy as jnp
from jax import lax
from jax.experimental import pallas as pl
from jax.experimental.pallas import tpu as pltpu
from jax.sharding import PartitionSpec as P

F32, BF16 = jnp.float32, jnp.bfloat16
V, L, F, R, C = 4, 37, 148, 64, 128
LQ = 10
E = 72
BW, BF, BZ, BN = 592, 816, 964, 976
PITCH = 158
KP = 160
OFF4, OFF3, OFF1 = 4, 5, 7
THIRD = 1.0 / 3.0


def iota(shape, dim):
    return lax.broadcasted_iota(jnp.int32, shape, dim)


def ns_pack(s0, s7, w0, w7, f0, f3, z0, z7, down, up):
    for f in range(F):
        down[f * 4 : f * 4 + 4, :] = s0[f, 0:4, :]
        up[f * 4 : f * 4 + 4, :] = s7[f, 4:8, :]
    for w in range(2 * L):
        down[BW + w * 3 : BW + w * 3 + 3, :] = w0[w, 0:3, :]
        up[BW + w * 3 : BW + w * 3 + 3, :] = w7[w, 5:8, :]
    for f in range(F):
        down[BF + f : BF + f + 1, :] = f0[f].astype(F32)[0:1]
        up[BF + f : BF + f + 1, :] = f3[f].astype(F32)[15:16]
    pad = jnp.zeros((BN - BZ - 1, C), F32)
    down[BZ:BN, :] = jnp.concatenate([z0[...].astype(F32)[0:1] * 0.1, pad], axis=0)
    up[BZ:BN, :] = jnp.concatenate([z7[...].astype(F32)[7:8] * 0.1, pad], axis=0)


def pack_north_south(state, wind, forcing, zone):
    st = jax.ShapeDtypeStruct((BN, C), F32)
    full = pl.BlockSpec((BN, C), lambda i: (0, 0))
    return pl.pallas_call(
        ns_pack,
        grid=(1,),
        out_shape=(st, st),
        in_specs=[
            pl.BlockSpec((F, 8, C), lambda i: (0, 0, 0)),
            pl.BlockSpec((F, 8, C), lambda i: (0, 7, 0)),
            pl.BlockSpec((2 * L, 8, C), lambda i: (0, 0, 0)),
            pl.BlockSpec((2 * L, 8, C), lambda i: (0, 7, 0)),
            pl.BlockSpec((F, 16, C), lambda i: (0, 0, 0)),
            pl.BlockSpec((F, 16, C), lambda i: (0, 3, 0)),
            pl.BlockSpec((8, C), lambda i: (0, 0)),
            pl.BlockSpec((8, C), lambda i: (7, 0)),
        ],
        out_specs=(full, full),
        compiler_params=pltpu.CompilerParams(vmem_limit_bytes=52 << 20),
        name="ns_pack",
    )(state, state, wind, wind, forcing, forcing, zone, zone)


def selector(j, ring):
    lane = iota((C, C), 1)
    col = iota((C, C), 0)
    pos = lane % 32
    if ring:
        want = jnp.where(pos == 11, 127, jnp.where(pos == 20, 0, -1))
    else:
        want = jnp.where(pos < 12, 116 + pos, jnp.where(pos >= 20, pos - 20, -1))
    return jnp.where((want == col) & (lane // 32 == j), 1.0, 0.0).astype(BF16)


def split(x):
    hi = x.astype(BF16)
    lo = (x - hi.astype(F32)).astype(BF16)
    return hi, lo


def fill_selectors(sel, rsel):
    for j in range(4):
        one = selector(j, False)
        sel[2 * j * C : (2 * j + 1) * C, :] = one
        sel[(2 * j + 1) * C : (2 * j + 2) * C, :] = one
        rsel[j * C : (j + 1) * C, :] = selector(j, True)


def fetch(srcs, dsts, sems, first=0):
    copies = [pltpu.make_async_copy(a, b, sems.at[first + i]) for i, (a, b) in enumerate(zip(srcs, dsts))]
    for c in copies:
        c.start()
    return copies


def done(copies):
    for c in copies:
        c.wait()


def stack(parts):
    return parts[0] if len(parts) == 1 else jnp.concatenate(parts, axis=0)


def strip_of(get, keys, sel):
    wide = []
    for j in range(4):
        wide += list(split(stack([get(key, j) for key in keys])))
    return jnp.dot(jnp.concatenate(wide, axis=1), sel[...], preferred_element_type=F32)


def ring_of(get, keys, rsel):
    wide = [stack([get(key, j) for key in keys]).astype(BF16) for j in range(4)]
    return jnp.dot(jnp.concatenate(wide, axis=1), rsel[...], preferred_element_type=F32)


def zone_lanes(zed, last_column):
    to = 8 + OFF1 if last_column else 8
    only = jnp.where(iota(zed.shape, 1) == to, pltpu.roll(zed, to + 1 if last_column else to, 1), 0.0)
    tot = only
    for j in range(1, 4):
        tot = tot + pltpu.roll(only, j * 32, 1)
    return tot


def put_strips(old, width, start, parts, off):
    lane = iota(parts[0][1].shape, 1)
    for q, s in parts:
        inside = (lane + (2 * C - off) - q * width) % 32 < width
        old = jnp.where(inside, pltpu.roll(s, (q * width + off - start + C) % C, 1), old)
    return old


def prepare(first_t, land_t, terrain_t, wb):
    zero = jnp.zeros((KP - F, 256), F32)
    extra = jnp.concatenate([land_t[...].astype(F32), terrain_t[...].astype(F32), zero[:2]], axis=0)
    for b in range(3):
        tall = []
        for a in range(3):
            tall += [first_t[3 * a + b].astype(F32), extra if (a == 1 and b == 1) else zero]
        wb[b] = jnp.concatenate(tall, axis=0).T.astype(BF16)


def ew_pack(state, wind, forcing, zone, first_t, land_t, terrain_t, strips, wstrips, east, west, wb, sel, rsel):
    lg = pl.program_id(0)

    @pl.when(lg == 0)
    def _():
        fill_selectors(sel, rsel)
        zed = zone[...].astype(F32) * 0.1
        for ref, at_end in ((east, True), (west, False)):
            ref[...] = jnp.zeros((9, R, C), F32)
            ref[8] = zone_lanes(zed, at_end)
        prepare(first_t, land_t, terrain_t, wb)

    def clean(x, i):
        return x if i < 5 else jnp.where(lg * 8 + i < L, x, 0.0)

    keys = [(m, v) for m in range(2) for v in range(V)]
    wkeys = [(m, c) for m in range(2) for c in range(2)]
    s = strip_of(lambda k, j: clean(state[k[1], k[0] * 4 + j], k[0] * 4 + j), keys, sel)
    f = ring_of(lambda k, j: clean(forcing[k[1], k[0] * 4 + j].astype(F32), k[0] * 4 + j), keys, rsel)
    w = strip_of(lambda k, j: clean(wind[k[1], k[0] * 4 + j], k[0] * 4 + j), wkeys, sel)
    pk = 7 + lg // 4
    for q, (m, v) in enumerate(keys):
        strips[m, v] = s[q * R : q * R + R]
    for n, (m, c) in enumerate(wkeys):
        wstrips[m, c] = w[n * R : n * R + R]
    for i in range(8):
        rows = slice(i * 8, i * 8 + 8)

        def cut(val, n):
            return val[n * R + i * 8 : n * R + i * 8 + 8]

        for ref, at4, at1, at3, on in ((east, 8, 11, 9, 1), (west, 20, 20, 20, 0)):
            ref[lg, rows, :] = put_strips(jnp.zeros((8, C), F32), 4, at4, [(q, cut(s, q)) for q in range(8)], on * OFF4)
            ref[pk, rows, :] = put_strips(
                ref[pk, rows, :], 1, at1, [((lg % 4) * 8 + q, cut(f, q)) for q in range(8)], on * OFF1
            )
            for c in range(2):
                ref[5 + c, rows, :] = put_strips(
                    ref[5 + c, rows, :], 3, at3, [(lg * 2 + m, cut(w, m * 2 + c)) for m in range(2)], on * OFF3
                )


def ew_pack_halo(below_any, above_any, s_in, w_in, e_in, x_in, strips, wstrips, east, west, sel, rsel, below, above, sems):
    get = fetch((below_any, above_any), (below, above), sems)
    fill_selectors(sel, rsel)
    done(get)
    zero = jnp.zeros((8, C), F32)

    def single(row):
        return jnp.concatenate([above[row : row + 1, :], zero[:6], below[row : row + 1, :]], axis=0)

    def four(row):
        return jnp.concatenate([above[row : row + 4, :], below[row : row + 4, :]], axis=0)

    def three(row):
        return jnp.concatenate([above[row : row + 3, :], zero[:2], below[row : row + 3, :]], axis=0)

    def state_at(k, j):
        level = k[0] * 4 + j
        return four((k[1] * L + level) * 4) if level < L else zero

    def wind_at(k, j):
        level = k[0] * 4 + j
        return three(BW + (k[1] * L + level) * 3) if level < L else zero

    def force_at(k, j):
        level = k[0] * 4 + j
        return single(BF + k[1] * L + level) if level < L else zero

    keys = [(m, v) for m in range(LQ) for v in range(V)]
    wkeys = [(m, c) for m in range(LQ) for c in range(2)]
    s = strip_of(state_at, keys, sel)
    f = ring_of(force_at, keys, rsel)
    w = strip_of(wind_at, wkeys, sel)
    zed = single(BZ)

    def cut(val, n):
        return val[n * 8 : n * 8 + 8]

    for n, (m, v) in enumerate(keys):
        strips[m, v] = cut(s, n)
    for n, (m, c) in enumerate(wkeys):
        wstrips[m, c] = cut(w, n)
    for ref, at_end, at4, at1, at3, on in ((east, True, 8, 11, 9, 1), (west, False, 20, 20, 20, 0)):
        for p in range(5):
            ref[p] = put_strips(zero, 4, at4, [(q, cut(s, p * 8 + q)) for q in range(8)], on * OFF4)
        for c in range(2):
            ref[5 + c] = put_strips(zero, 3, at3, [(m, cut(w, m * 2 + c)) for m in range(LQ)], on * OFF3)
        ref[7] = put_strips(zero, 1, at1, [(q, cut(f, q)) for q in range(32)], on * OFF1)
        ref[8] = put_strips(zone_lanes(zed, at_end), 1, at1, [(q, cut(f, 32 + q)) for q in range(8)], on * OFF1)


NS_SCRATCH = [pltpu.VMEM((BN, C), F32), pltpu.VMEM((BN, C), F32), pltpu.SemaphoreType.DMA((2,))]
SELECTORS = [pltpu.VMEM((8 * C, C), BF16), pltpu.VMEM((4 * C, C), BF16)]
PACKED = (
    jax.ShapeDtypeStruct((LQ, V, E, C), F32),
    jax.ShapeDtypeStruct((LQ, 2, E, C), F32),
    jax.ShapeDtypeStruct((9, E, C), F32),
    jax.ShapeDtypeStruct((9, E, C), F32),
)


def pack_east_west(state, wind, forcing, zone, first_t, land_t, terrain_t):
    return pl.pallas_call(
        ew_pack,
        grid=(5,),
        out_shape=PACKED + (jax.ShapeDtypeStruct((3, 256, 3 * KP), BF16),),
        in_specs=[
            pl.BlockSpec((V, 8, R, C), lambda i: (0, i, 0, 0)),
            pl.BlockSpec((2, 8, R, C), lambda i: (0, i, 0, 0)),
            pl.BlockSpec((V, 8, R, C), lambda i: (0, i, 0, 0)),
            pl.BlockSpec((R, C), lambda i: (0, 0)),
            pl.BlockSpec(first_t.shape, lambda i: (0, 0, 0)),
            pl.BlockSpec(land_t.shape, lambda i: (0, 0)),
            pl.BlockSpec(terrain_t.shape, lambda i: (0, 0)),
        ],
        out_specs=(
            pl.BlockSpec((2, V, R, C), lambda i: (i, 0, 0, 0)),
            pl.BlockSpec((2, 2, R, C), lambda i: (i, 0, 0, 0)),
            pl.BlockSpec((9, R, C), lambda i: (0, 0, 0)),
            pl.BlockSpec((9, R, C), lambda i: (0, 0, 0)),
            pl.BlockSpec((3, 256, 3 * KP), lambda i: (0, 0, 0)),
        ),
        scratch_shapes=SELECTORS,
        compiler_params=pltpu.CompilerParams(vmem_limit_bytes=32 << 20),
        cost_estimate=pl.CostEstimate(flops=4_000_000_000, bytes_accessed=13_000_000, transcendentals=0),
        name="ew_pack",
    )(state, wind, forcing, zone, first_t, land_t, terrain_t)


def pack_halo(below, above, packed):
    hbm = pl.BlockSpec(memory_space=pl.ANY)
    return pl.pallas_call(
        ew_pack_halo,
        grid=(1,),
        out_shape=PACKED,
        in_specs=[hbm] * 6,
        out_specs=(
            pl.BlockSpec((LQ, V, 8, C), lambda i: (0, 0, 8, 0)),
            pl.BlockSpec((LQ, 2, 8, C), lambda i: (0, 0, 8, 0)),
            pl.BlockSpec((9, 8, C), lambda i: (0, 8, 0)),
            pl.BlockSpec((9, 8, C), lambda i: (0, 8, 0)),
        ),
        scratch_shapes=SELECTORS + NS_SCRATCH,
        input_output_aliases={2: 0, 3: 1, 4: 2, 5: 3},
        compiler_params=pltpu.CompilerParams(vmem_limit_bytes=24 << 20),
        name="ew_pack_halo",
    )(below, above, *packed)


def put_ring(ref, v, i, val):
    ref[v, i * 8 : i * 8 + 8, :] = val


class Around:
    def __init__(self, ref):
        self.ref, self.have = ref, {}
        row = iota((8, C), 0)
        self.top, self.bottom = row == 7, row == 0

    def block(self, v, i):
        i = i % 9 + (9 if i == 9 else 0)
        if (v, i) not in self.have:
            k = i % 9
            q = self.ref[v, k * 8 : k * 8 + 8, :]
            self.have[v, i] = (q, pltpu.roll(q, 7, 0), pltpu.roll(q, 1, 0))
        return self.have[v, i]

    def __call__(self, v, i):
        if i == 0:
            q8 = self.ref[v, 64:72, :]
            before = pltpu.roll(q8, 1, 0)
        else:
            before = self.block(v, i - 1)[2]
        q, up, dn = self.block(v, i)
        n = jnp.where(self.top, self.block(v, i + 1)[1], up)
        s = jnp.where(self.bottom, before, dn)
        return q, pltpu.roll(q, C - 1, 1), pltpu.roll(q, 1, 1), n, s


def stage_three(f2, c2, w2, emit):
    at = Around(f2)
    for i in range(9):
        rows = slice(i * 8, i * 8 + 8)
        ce, cw, cn, cs = (w2[k, rows, :] for k in range(4))
        for v in range(V):
            q, e, w, n, s = at(v, i)
            g = (ce * e + cw * w) + (cn * n + cs * s)
            emit(v, i, THIRD * c2[v, rows, :] + (2.0 * THIRD) * (0.6 * q + g))


def stage_two(f1, c1, w1, f2, c2, w2):
    at = Around(f1)
    for i in range(9):
        rows = slice(i * 8, i * 8 + 8)
        ce, cw, cn, cs = (w1[k, rows, :] for k in range(4))
        for v in range(V):
            q, e, w, n, s = at(v, i)
            g = (ce * e + cw * w) + (cn * n + cs * s)
            c = c1[v, rows, :]
            c2[v, rows, :] = c
            put_ring(f2, v, i, 0.75 * c + 0.25 * (0.6 * q + g))
        for k, val in enumerate((ce, cw, cn, cs)):
            w2[k, rows, :] = val


def stage_one(x, wind_at, diff, f1, c1, w1):
    at = Around(x)
    for i in range(9):
        rows = slice(i * 8, i * 8 + 8)
        d = diff[rows, :]
        hu, hv = (0.5 * wind_at(k, i) for k in range(2))
        ce, cw, cn, cs = d - hu, d + hu, d - hv, d + hv
        for v in range(V):
            q, e, w, n, s = at(v, i)
            g = (ce * e + cw * w) + (cn * n + cs * s)
            c1[v, rows, :] = q
            put_ring(f1, v, i, 0.6 * q + g)
        for k, val in enumerate((ce, cw, cn, cs)):
            w1[k, rows, :] = val


def diffusion(strip):
    row, lane = iota((E, C), 0), iota((E, C), 1)
    gy, gx = lax.axis_index("gy"), lax.axis_index("gx")
    ok_above = jnp.where(gy < lax.axis_size("gy") - 1, 1, 0)
    ok_below = jnp.where(gy > 0, 1, 0)
    ok = jnp.where(row < 64, 1, jnp.where(row < 68, ok_above, ok_below))
    if strip:
        pos = lane % 32
        ok_east = jnp.where(gx < lax.axis_size("gx") - 1, 1, 0)
        ok_west = jnp.where(gx > 0, 1, 0)
        ok = ok * jnp.where((pos >= 12) & (pos < 16), ok_east, jnp.where((pos >= 16) & (pos < 20), ok_west, 1))
    return 0.1 * ok.astype(F32)


def stage_scratch():
    return [
        pltpu.VMEM((V, E, C), F32),
        pltpu.VMEM((V, E, C), F32),
        pltpu.VMEM((V, E, C), F32),
        pltpu.VMEM((V, E, C), F32),
        pltpu.VMEM((V, E, C), F32),
        pltpu.VMEM((4, E, C), F32),
        pltpu.VMEM((4, E, C), F32),
        pltpu.VMEM((E, C), F32),
    ]


def main_stages(state, wind, below, above, third, x, f1, f2, c1, c2, w1, w2, diff):
    block = pl.program_id(0)

    @pl.when(block == 0)
    def _():
        diff[...] = diffusion(False)

    def one(k, carry):
        level = jnp.minimum(block * 8 + k, L - 1)

        def emit(v, i, val):
            third[v, k, i * 8 : i * 8 + 8, :] = val

        stage_three(f2, c2, w2, emit)
        stage_two(f1, c1, w1, f2, c2, w2)
        for v in range(V):
            for i in range(8):
                put_ring(x, v, i, state[v, k, i * 8 : i * 8 + 8, :])
            at = pl.ds((v * L + level) * 4, 4)
            put_ring(x, v, 8, jnp.concatenate([above[at, :], below[at, :]], axis=0))

        def wind_at(c, i):
            if i < 8:
                return wind[c, k, i * 8 : i * 8 + 8, :]
            at = pl.ds(BW + (c * L + level) * 3, 3)
            return jnp.concatenate([above[at, :], jnp.zeros((2, C), F32), below[at, :]], axis=0)

        stage_one(x, wind_at, diff, f1, c1, w1)
        return carry

    lax.fori_loop(0, 8, one, 0, unroll=4)


def run_main(state, wind, below, above):
    return pl.pallas_call(
        main_stages,
        grid=(5,),
        out_shape=jax.ShapeDtypeStruct((V, 40, E, C), F32),
        in_specs=[
            pl.BlockSpec((V, 8, R, C), lambda i: (0, i, 0, 0)),
            pl.BlockSpec((2, 8, R, C), lambda i: (0, i, 0, 0)),
            pl.BlockSpec((BN, C), lambda i: (0, 0)),
            pl.BlockSpec((BN, C), lambda i: (0, 0)),
        ],
        out_specs=pl.BlockSpec((V, 8, E, C), lambda i: (0, i, 0, 0)),
        scratch_shapes=stage_scratch(),
        compiler_params=pltpu.CompilerParams(vmem_limit_bytes=24 << 20),
        cost_estimate=pl.CostEstimate(flops=60_000_000, bytes_accessed=13_000_000, transcendentals=0),
        name="main_stages",
    )(state, wind, below, above)


def silu(v):
    h = 0.5 * v
    return h + h * jnp.tanh(h)


def last(*refs):
    ins, out_any, bufs = refs[:14], refs[14], refs[15:29]
    (x, f1, f2, c1, c2, w1, w2, diff, sr, zs, zx, y0, yf, b0, bm, bp, h1, h2, sems) = refs[29:]
    (strips, wstrips, fromw, frome, zone, below, above, third, forcing, land, terrain, wb, w2t, w3t) = bufs
    edge = pl.ds(BF, BN - BF)
    edges = list(ins[:5]) + [ins[5].at[edge, :], ins[6].at[edge, :]]
    done(fetch(edges, bufs[:7], sems))
    get_main = fetch(ins[7:11], bufs[7:11], sems, 7)
    get_weights = fetch(ins[11:], bufs[11:], sems, 11)
    lane = iota((8, C), 1)
    pos = lane % 32

    def unpack(p, rows, start, width):
        mine = (lane + 2 * C - start) % 32 < width
        return pltpu.roll(jnp.where(mine, frome[p, rows, :], fromw[p, rows, :]), (12 - start + C) % C, 1)

    diff[...] = diffusion(True)
    zx[0:64, :] = zone[...].astype(F32) * 0.1
    zx[64:72, :] = jnp.concatenate(
        [above[BZ - BF : BZ - BF + 1, :], jnp.zeros((6, C), F32), below[BZ - BF : BZ - BF + 1, :]], axis=0
    )
    for i in range(9):
        rows = slice(i * 8, i * 8 + 8)
        zs[rows, :] = jnp.where((pos == 19) | (pos == 12), unpack(8, rows, 8, 1), 0.0)

    in_halo = (pos >= 12) & (pos < 20)

    def strip_step(step, carry):
        lq2 = jnp.maximum(step - 2, 0)
        lq = jnp.minimum(step, LQ - 1)
        pk2 = 7 + lq2 // 8

        def emit(v, i, val):
            rows = slice(i * 8, i * 8 + 8)
            q = (lq2 % 8) * 4 + v
            sr[lq2, v, rows, :] = val + zs[rows, :] * (unpack(pk2, rows, q, 1) - val)

        stage_three(f2, c2, w2, emit)
        stage_two(f1, c1, w1, f2, c2, w2)
        pk = lq // 2
        for v in range(V):
            q4 = ((lq % 2) * 4 + v) * 4
            for i in range(9):
                rows = slice(i * 8, i * 8 + 8)
                put_ring(x, v, i, jnp.where(in_halo, unpack(pk, rows, q4, 4), strips[lq, v, rows, :]))

        def wind_at(k, i):
            rows = slice(i * 8, i * 8 + 8)
            return jnp.where(in_halo, unpack(5 + k, rows, lq * 3, 3), wstrips[lq, k, rows, :])

        stage_one(x, wind_at, diff, f1, c1, w1)
        return carry

    lax.fori_loop(0, LQ + 2, strip_step, 0)

    done(get_main)
    lo, hi = lane <= 2, lane >= 125

    def merge_one(v, lq, j):
        level = lq * 4 + j
        f = v * L + level
        fmain = forcing[v, level].astype(F32)
        for i in range(9):
            rows = slice(i * 8, i * 8 + 8)
            s = sr[lq, v, rows, :]
            te = pltpu.roll(s, (127 - (j * 32 + 11)) % C, 1)
            tw = pltpu.roll(s, (-(j * 32 + 20)) % C, 1)
            t = jnp.where(lo, tw, jnp.where(hi, te, third[v, level + 2, rows, :]))
            if i < 8:
                fv = fmain[i * 8 : i * 8 + 8]
            else:
                fv = jnp.concatenate(
                    [above[pl.ds(f, 1), :], jnp.zeros((6, C), F32), below[pl.ds(f, 1), :]], axis=0
                )
            r = t + zx[rows, :] * (fv - t)
            at = pl.ds((i * 8 + 1) * PITCH + f, 8, stride=PITCH)
            y0[at, :] = r
            yf[at, :] = jnp.where(lane == 127, tw, te)

    def merge(lq, carry):
        for v in range(V):
            for j in range(4):
                merge_one(v, lq, j)
        return carry

    lax.fori_loop(0, LQ - 1, merge, 0)
    for v in range(V):
        merge_one(v, LQ - 1, 0)

    def hot(yb, carry):
        lnd = land[pl.ds(yb * 8, 8), :]
        ter = terrain[pl.ds(yb * 8, 8), :]
        for k in range(8):
            j = iota((16, C), 0)
            oh = jnp.where(j < 2, jnp.where(j == lnd[k : k + 1], 1.0, 0.0), jnp.where(j - 2 == ter[k : k + 1], 1.0, 0.0))
            base = (yb * 8 + k + 1) * PITCH + F
            y0[pl.ds(base, 10), :] = oh[0:10]
            yf[pl.ds(base, 10), :] = jnp.zeros((10, C), F32)
        return carry

    lax.fori_loop(0, 8, hot, 0)
    for ref in (y0, yf):
        for p in (65, 72):
            ref[p * PITCH + F : p * PITCH + F + 10, :] = jnp.zeros((10, C), F32)
        ref[73 * PITCH : 73 * PITCH + 8, :] = jnp.zeros((8, C), F32)
        ref[66 * PITCH : 66 * PITCH + 8, :] = jnp.zeros((8, C), F32)

    def convert(p):
        src = jnp.where(p == 0, 72, p) * PITCH
        dst = pl.multiple_of(p * KP, 16)
        own, outer = y0[pl.ds(src, KP), :], yf[pl.ds(src, KP), :]
        wide = iota((KP, C), 1)
        b0[pl.ds(dst, KP), :] = own.astype(BF16)
        bm[pl.ds(dst, KP), :] = pltpu.roll(jnp.where(wide == 127, outer, own), 1, 1).astype(BF16)
        bp[pl.ds(dst, KP), :] = pltpu.roll(jnp.where(wide == 0, outer, own), C - 1, 1).astype(BF16)

    for p in range(4):
        convert(p)
    done(get_weights)

    def network(t, carry):
        a2 = silu(h2[...]).astype(BF16)
        a1 = silu(h1[...]).astype(BF16)
        tc = jnp.minimum(t, R // 2 - 1)
        acc = None
        for k, b in enumerate((bm, b0, bp)):
            pair = jnp.concatenate(
                [b[pl.ds(pl.multiple_of((2 * tc + u) * KP, 16), 3 * KP), :] for u in range(2)], axis=1
            )
            d = jnp.dot(wb[k], pair, preferred_element_type=F32)
            acc = d if acc is None else acc + d
        for u in range(2):
            convert(jnp.minimum(2 * t + 4 + u, 65))
        h1[...] = acc
        h2[...] = jnp.dot(w2t[...], a1, preferred_element_type=F32)
        ph = jnp.dot(w3t[...], a2, preferred_element_type=F32)
        base = jnp.where(t >= 2, 2 * t - 3, 66)
        for u in range(2):
            at = pl.ds((base + u) * PITCH, F)
            y0[at, :] = y0[at, :] + ph[:F, u * C : u * C + C]
        return carry

    def put(j, v):
        rows = pl.ds(pl.multiple_of(j * 8, 8), 8)
        src = third.at[v, pl.ds(0, L), rows, :]
        return pltpu.make_async_copy(src, out_any.at[pl.ds(v * L, L), rows, :], sems.at[14 + 4 * j + v])

    def write(j):
        rows = pl.ds(pl.multiple_of(j * 8, 8), 8)
        for f in range(F):
            third[f // L, f % L, rows, :] = y0[pl.ds((j * 8 + 1) * PITCH + f, 8, stride=PITCH), :]
        for v in range(V):
            put(j, v).start()

    def rows_of_eight(j, carry):
        write(j - 1)
        for i in range(4):
            network(4 * j + 2 + i, 0)
        return carry

    lax.fori_loop(0, 6, network, 0, unroll=6)
    lax.fori_loop(1, R // 8, rows_of_eight, 0)
    write(R // 8 - 1)
    for j in range(R // 8):
        for v in range(V):
            put(j, v).wait()


def run_last(*args):
    n = 74 * PITCH
    hbm = pl.BlockSpec(memory_space=pl.ANY)
    shapes = [a.shape for a in args]
    shapes[5] = shapes[6] = (BN - BF, C)
    scratch = [pltpu.VMEM(shape, a.dtype) for shape, a in zip(shapes, args)] + stage_scratch()
    scratch += [
        pltpu.VMEM((LQ, V, E, C), F32),
        pltpu.VMEM((E, C), F32),
        pltpu.VMEM((E, C), F32),
    ]
    scratch += [pltpu.VMEM((n, C), F32)] * 2 + [pltpu.VMEM((66 * KP, C), BF16)] * 3
    scratch += [
        pltpu.VMEM((256, 256), F32),
        pltpu.VMEM((256, 256), F32),
        pltpu.SemaphoreType.DMA((14 + 4 * (R // 8),)),
    ]
    return pl.pallas_call(
        last,
        out_shape=jax.ShapeDtypeStruct((F, R, C), F32),
        in_specs=[hbm] * len(args),
        out_specs=hbm,
        scratch_shapes=scratch,
        compiler_params=pltpu.CompilerParams(vmem_limit_bytes=38 << 20),
        cost_estimate=pl.CostEstimate(flops=9_000_000_000, bytes_accessed=20_000_000, transcendentals=4_000_000),
        name="strips_and_network",
    )(*args)


def local(state, wind, forcing, zone, land, terrain, first_weight, second_weight, third_weight, land_embed, terrain_embed):
    def shifts(axis):
        size = lax.axis_size(axis)
        up = [(i, i + 1) for i in range(size - 1)]
        return up, [(j, i) for i, j in up]

    down_buf, up_buf = pack_north_south(state, wind.reshape(2 * L, R, C), forcing, zone)
    up, down = shifts("gy")
    below = lax.ppermute(up_buf, "gy", up)
    above = lax.ppermute(down_buf, "gy", down)

    shaped = state.reshape(V, L, R, C)
    forced = forcing.reshape(V, L, R, C)
    packed = pack_east_west(shaped, wind, forced, zone, first_weight.transpose(0, 2, 1), land_embed.T, terrain_embed.T)
    wb = packed[4]
    strips, wstrips, east, west = pack_halo(below, above, packed[:4])
    up, down = shifts("gx")
    fromw = lax.ppermute(east, "gx", up)
    frome = lax.ppermute(west, "gx", down)
    third = run_main(shaped, wind, below, above)
    return run_last(
        strips, wstrips, fromw, frome, zone, below, above, third, forced, land, terrain, wb, second_weight, third_weight
    )


def solution(mesh):
    in_specs = (
        P(None, "gy", "gx"),
        P(None, None, "gy", "gx"),
        P(None, "gy", "gx"),
        P("gy", "gx"),
        P("gy", "gx"),
        P("gy", "gx"),
        P(),
        P(),
        P(),
        P(),
        P(),
    )
    out_specs = P(None, "gy", "gx")
    return jax.shard_map(local, mesh=mesh, in_specs=in_specs, out_specs=out_specs, check_vma=False)
```

```python
import jax
import jax.numpy as jnp
from jax import lax
from jax.experimental import pallas as pl
from jax.experimental.pallas import tpu as pltpu
from jax.sharding import PartitionSpec as P

F32, BF16 = jnp.float32, jnp.bfloat16
V, L, F, R, C = 4, 37, 148, 64, 128
LQ = 10
E = 72
BW, BF, BZ, BN = 592, 816, 964, 976
PITCH = 158
KP = 160
OFF4, OFF3, OFF1 = 4, 5, 7
THIRD = 1.0 / 3.0


def iota(shape, dim):
    return lax.broadcasted_iota(jnp.int32, shape, dim)


def ns_pack(s0, s7, w0, w7, f0, f3, z0, z7, down, up):
    for f in range(F):
        down[f * 4 : f * 4 + 4, :] = s0[f, 0:4, :]
        up[f * 4 : f * 4 + 4, :] = s7[f, 4:8, :]
    for w in range(2 * L):
        down[BW + w * 3 : BW + w * 3 + 3, :] = w0[w, 0:3, :]
        up[BW + w * 3 : BW + w * 3 + 3, :] = w7[w, 5:8, :]
    for f in range(F):
        down[BF + f : BF + f + 1, :] = f0[f].astype(F32)[0:1]
        up[BF + f : BF + f + 1, :] = f3[f].astype(F32)[15:16]
    pad = jnp.zeros((BN - BZ - 1, C), F32)
    down[BZ:BN, :] = jnp.concatenate([z0[...].astype(F32)[0:1] * 0.1, pad], axis=0)
    up[BZ:BN, :] = jnp.concatenate([z7[...].astype(F32)[7:8] * 0.1, pad], axis=0)


def pack_north_south(state, wind, forcing, zone):
    st = jax.ShapeDtypeStruct((BN, C), F32)
    full = pl.BlockSpec((BN, C), lambda i: (0, 0))
    return pl.pallas_call(
        ns_pack,
        grid=(1,),
        out_shape=(st, st),
        in_specs=[
            pl.BlockSpec((F, 8, C), lambda i: (0, 0, 0)),
            pl.BlockSpec((F, 8, C), lambda i: (0, 7, 0)),
            pl.BlockSpec((2 * L, 8, C), lambda i: (0, 0, 0)),
            pl.BlockSpec((2 * L, 8, C), lambda i: (0, 7, 0)),
            pl.BlockSpec((F, 16, C), lambda i: (0, 0, 0)),
            pl.BlockSpec((F, 16, C), lambda i: (0, 3, 0)),
            pl.BlockSpec((8, C), lambda i: (0, 0)),
            pl.BlockSpec((8, C), lambda i: (7, 0)),
        ],
        out_specs=(full, full),
        compiler_params=pltpu.CompilerParams(vmem_limit_bytes=52 << 20),
        name="ns_pack",
    )(state, state, wind, wind, forcing, forcing, zone, zone)


def selector(j, ring):
    lane = iota((C, C), 1)
    col = iota((C, C), 0)
    pos = lane % 32
    if ring:
        want = jnp.where(pos == 11, 127, jnp.where(pos == 20, 0, -1))
    else:
        want = jnp.where(pos < 12, 116 + pos, jnp.where(pos >= 20, pos - 20, -1))
    return jnp.where((want == col) & (lane // 32 == j), 1.0, 0.0).astype(BF16)


def split(x):
    hi = x.astype(BF16)
    lo = (x - hi.astype(F32)).astype(BF16)
    return hi, lo


def fill_selectors(sel, rsel):
    for j in range(4):
        one = selector(j, False)
        sel[2 * j * C : (2 * j + 1) * C, :] = one
        sel[(2 * j + 1) * C : (2 * j + 2) * C, :] = one
        rsel[j * C : (j + 1) * C, :] = selector(j, True)


def fetch(srcs, dsts, sems, first=0):
    copies = [pltpu.make_async_copy(a, b, sems.at[first + i]) for i, (a, b) in enumerate(zip(srcs, dsts))]
    for c in copies:
        c.start()
    return copies


def done(copies):
    for c in copies:
        c.wait()


def stack(parts):
    return parts[0] if len(parts) == 1 else jnp.concatenate(parts, axis=0)


def strip_of(get, keys, sel):
    wide = []
    for j in range(4):
        wide += list(split(stack([get(key, j) for key in keys])))
    return jnp.dot(jnp.concatenate(wide, axis=1), sel[...], preferred_element_type=F32)


def ring_of(get, keys, rsel):
    wide = [stack([get(key, j) for key in keys]).astype(BF16) for j in range(4)]
    return jnp.dot(jnp.concatenate(wide, axis=1), rsel[...], preferred_element_type=F32)


def zone_lanes(zed, last_column):
    to = 8 + OFF1 if last_column else 8
    only = jnp.where(iota(zed.shape, 1) == to, pltpu.roll(zed, to + 1 if last_column else to, 1), 0.0)
    tot = only
    for j in range(1, 4):
        tot = tot + pltpu.roll(only, j * 32, 1)
    return tot


def put_strips(old, width, start, parts, off):
    lane = iota(parts[0][1].shape, 1)
    for q, s in parts:
        inside = (lane + (2 * C - off) - q * width) % 32 < width
        old = jnp.where(inside, pltpu.roll(s, (q * width + off - start + C) % C, 1), old)
    return old


def prepare(first_t, land_t, terrain_t, wb):
    zero = jnp.zeros((KP - F, 256), F32)
    extra = jnp.concatenate([land_t[...].astype(F32), terrain_t[...].astype(F32), zero[:2]], axis=0)
    for b in range(3):
        tall = []
        for a in range(3):
            tall += [first_t[3 * a + b].astype(F32), extra if (a == 1 and b == 1) else zero]
        wb[:, b * 3 * KP : (b + 1) * 3 * KP] = jnp.concatenate(tall, axis=0).T.astype(BF16)


def ew_pack(state, wind, forcing, zone, first_t, land_t, terrain_t, strips, wstrips, east, west, wb, sel, rsel):
    lg = pl.program_id(0)

    @pl.when(lg == 0)
    def _():
        fill_selectors(sel, rsel)
        zed = zone[...].astype(F32) * 0.1
        for ref, at_end in ((east, True), (west, False)):
            ref[...] = jnp.zeros((9, R, C), F32)
            ref[8] = zone_lanes(zed, at_end)
        prepare(first_t, land_t, terrain_t, wb)

    def clean(x, i):
        return x if i < 5 else jnp.where(lg * 8 + i < L, x, 0.0)

    keys = [(m, v) for m in range(2) for v in range(V)]
    wkeys = [(m, c) for m in range(2) for c in range(2)]
    s = strip_of(lambda k, j: clean(state[k[1], k[0] * 4 + j], k[0] * 4 + j), keys, sel)
    f = ring_of(lambda k, j: clean(forcing[k[1], k[0] * 4 + j].astype(F32), k[0] * 4 + j), keys, rsel)
    w = strip_of(lambda k, j: clean(wind[k[1], k[0] * 4 + j], k[0] * 4 + j), wkeys, sel)
    pk = 7 + lg // 4
    for q, (m, v) in enumerate(keys):
        strips[m, v] = s[q * R : q * R + R]
    for n, (m, c) in enumerate(wkeys):
        wstrips[m, c] = w[n * R : n * R + R]
    for i in range(8):
        rows = slice(i * 8, i * 8 + 8)

        def cut(val, n):
            return val[n * R + i * 8 : n * R + i * 8 + 8]

        for ref, at4, at1, at3, on in ((east, 8, 11, 9, 1), (west, 20, 20, 20, 0)):
            ref[lg, rows, :] = put_strips(jnp.zeros((8, C), F32), 4, at4, [(q, cut(s, q)) for q in range(8)], on * OFF4)
            ref[pk, rows, :] = put_strips(
                ref[pk, rows, :], 1, at1, [((lg % 4) * 8 + q, cut(f, q)) for q in range(8)], on * OFF1
            )
            for c in range(2):
                ref[5 + c, rows, :] = put_strips(
                    ref[5 + c, rows, :], 3, at3, [(lg * 2 + m, cut(w, m * 2 + c)) for m in range(2)], on * OFF3
                )


def ew_pack_halo(below_any, above_any, s_in, w_in, e_in, x_in, strips, wstrips, east, west, sel, rsel, below, above, sems):
    get = fetch((below_any, above_any), (below, above), sems)
    fill_selectors(sel, rsel)
    done(get)
    zero = jnp.zeros((8, C), F32)

    def single(row):
        return jnp.concatenate([above[row : row + 1, :], zero[:6], below[row : row + 1, :]], axis=0)

    def four(row):
        return jnp.concatenate([above[row : row + 4, :], below[row : row + 4, :]], axis=0)

    def three(row):
        return jnp.concatenate([above[row : row + 3, :], zero[:2], below[row : row + 3, :]], axis=0)

    def state_at(k, j):
        level = k[0] * 4 + j
        return four((k[1] * L + level) * 4) if level < L else zero

    def wind_at(k, j):
        level = k[0] * 4 + j
        return three(BW + (k[1] * L + level) * 3) if level < L else zero

    def force_at(k, j):
        level = k[0] * 4 + j
        return single(BF + k[1] * L + level) if level < L else zero

    keys = [(m, v) for m in range(LQ) for v in range(V)]
    wkeys = [(m, c) for m in range(LQ) for c in range(2)]
    s = strip_of(state_at, keys, sel)
    f = ring_of(force_at, keys, rsel)
    w = strip_of(wind_at, wkeys, sel)
    zed = single(BZ)

    def cut(val, n):
        return val[n * 8 : n * 8 + 8]

    for n, (m, v) in enumerate(keys):
        strips[m, v] = cut(s, n)
    for n, (m, c) in enumerate(wkeys):
        wstrips[m, c] = cut(w, n)
    for ref, at_end, at4, at1, at3, on in ((east, True, 8, 11, 9, 1), (west, False, 20, 20, 20, 0)):
        for p in range(5):
            ref[p] = put_strips(zero, 4, at4, [(q, cut(s, p * 8 + q)) for q in range(8)], on * OFF4)
        for c in range(2):
            ref[5 + c] = put_strips(zero, 3, at3, [(m, cut(w, m * 2 + c)) for m in range(LQ)], on * OFF3)
        ref[7] = put_strips(zero, 1, at1, [(q, cut(f, q)) for q in range(32)], on * OFF1)
        ref[8] = put_strips(zone_lanes(zed, at_end), 1, at1, [(q, cut(f, 32 + q)) for q in range(8)], on * OFF1)


NS_SCRATCH = [pltpu.VMEM((BN, C), F32), pltpu.VMEM((BN, C), F32), pltpu.SemaphoreType.DMA((2,))]
SELECTORS = [pltpu.VMEM((8 * C, C), BF16), pltpu.VMEM((4 * C, C), BF16)]
PACKED = (
    jax.ShapeDtypeStruct((LQ, V, E, C), F32),
    jax.ShapeDtypeStruct((LQ, 2, E, C), F32),
    jax.ShapeDtypeStruct((9, E, C), F32),
    jax.ShapeDtypeStruct((9, E, C), F32),
)


def pack_east_west(state, wind, forcing, zone, first_t, land_t, terrain_t):
    return pl.pallas_call(
        ew_pack,
        grid=(5,),
        out_shape=PACKED + (jax.ShapeDtypeStruct((256, 9 * KP), BF16),),
        in_specs=[
            pl.BlockSpec((V, 8, R, C), lambda i: (0, i, 0, 0)),
            pl.BlockSpec((2, 8, R, C), lambda i: (0, i, 0, 0)),
            pl.BlockSpec((V, 8, R, C), lambda i: (0, i, 0, 0)),
            pl.BlockSpec((R, C), lambda i: (0, 0)),
            pl.BlockSpec(first_t.shape, lambda i: (0, 0, 0)),
            pl.BlockSpec(land_t.shape, lambda i: (0, 0)),
            pl.BlockSpec(terrain_t.shape, lambda i: (0, 0)),
        ],
        out_specs=(
            pl.BlockSpec((2, V, R, C), lambda i: (i, 0, 0, 0)),
            pl.BlockSpec((2, 2, R, C), lambda i: (i, 0, 0, 0)),
            pl.BlockSpec((9, R, C), lambda i: (0, 0, 0)),
            pl.BlockSpec((9, R, C), lambda i: (0, 0, 0)),
            pl.BlockSpec((256, 9 * KP), lambda i: (0, 0)),
        ),
        scratch_shapes=SELECTORS,
        compiler_params=pltpu.CompilerParams(vmem_limit_bytes=32 << 20),
        cost_estimate=pl.CostEstimate(flops=4_000_000_000, bytes_accessed=13_000_000, transcendentals=0),
        name="ew_pack",
    )(state, wind, forcing, zone, first_t, land_t, terrain_t)


def pack_halo(below, above, packed):
    hbm = pl.BlockSpec(memory_space=pl.ANY)
    return pl.pallas_call(
        ew_pack_halo,
        grid=(1,),
        out_shape=PACKED,
        in_specs=[hbm] * 6,
        out_specs=(
            pl.BlockSpec((LQ, V, 8, C), lambda i: (0, 0, 8, 0)),
            pl.BlockSpec((LQ, 2, 8, C), lambda i: (0, 0, 8, 0)),
            pl.BlockSpec((9, 8, C), lambda i: (0, 8, 0)),
            pl.BlockSpec((9, 8, C), lambda i: (0, 8, 0)),
        ),
        scratch_shapes=SELECTORS + NS_SCRATCH,
        input_output_aliases={2: 0, 3: 1, 4: 2, 5: 3},
        compiler_params=pltpu.CompilerParams(vmem_limit_bytes=24 << 20),
        name="ew_pack_halo",
    )(below, above, *packed)


def put_ring(ref, v, i, val):
    ref[v, i * 8 : i * 8 + 8, :] = val


class Around:
    def __init__(self, ref):
        self.ref, self.have = ref, {}
        row = iota((8, C), 0)
        self.top, self.bottom = row == 7, row == 0

    def block(self, v, i):
        i = i % 9 + (9 if i == 9 else 0)
        if (v, i) not in self.have:
            k = i % 9
            q = self.ref[v, k * 8 : k * 8 + 8, :]
            self.have[v, i] = (q, pltpu.roll(q, 7, 0), pltpu.roll(q, 1, 0))
        return self.have[v, i]

    def __call__(self, v, i):
        if i == 0:
            q8 = self.ref[v, 64:72, :]
            before = pltpu.roll(q8, 1, 0)
        else:
            before = self.block(v, i - 1)[2]
        q, up, dn = self.block(v, i)
        n = jnp.where(self.top, self.block(v, i + 1)[1], up)
        s = jnp.where(self.bottom, before, dn)
        return q, pltpu.roll(q, C - 1, 1), pltpu.roll(q, 1, 1), n, s


def stage_three(f2, c2, w2, emit):
    at = Around(f2)
    for i in range(9):
        rows = slice(i * 8, i * 8 + 8)
        ce, cw, cn, cs = (w2[k, rows, :] for k in range(4))
        for v in range(V):
            q, e, w, n, s = at(v, i)
            g = (ce * e + cw * w) + (cn * n + cs * s)
            emit(v, i, THIRD * c2[v, rows, :] + (2.0 * THIRD) * (0.6 * q + g))


def stage_two(f1, c1, w1, f2, c2, w2):
    at = Around(f1)
    for i in range(9):
        rows = slice(i * 8, i * 8 + 8)
        ce, cw, cn, cs = (w1[k, rows, :] for k in range(4))
        for v in range(V):
            q, e, w, n, s = at(v, i)
            g = (ce * e + cw * w) + (cn * n + cs * s)
            c = c1[v, rows, :]
            c2[v, rows, :] = c
            put_ring(f2, v, i, 0.75 * c + 0.25 * (0.6 * q + g))
        for k, val in enumerate((ce, cw, cn, cs)):
            w2[k, rows, :] = val


def stage_one(x, wind_at, diff, f1, c1, w1):
    at = Around(x)
    for i in range(9):
        rows = slice(i * 8, i * 8 + 8)
        d = diff[rows, :]
        hu, hv = (0.5 * wind_at(k, i) for k in range(2))
        ce, cw, cn, cs = d - hu, d + hu, d - hv, d + hv
        for v in range(V):
            q, e, w, n, s = at(v, i)
            g = (ce * e + cw * w) + (cn * n + cs * s)
            c1[v, rows, :] = q
            put_ring(f1, v, i, 0.6 * q + g)
        for k, val in enumerate((ce, cw, cn, cs)):
            w1[k, rows, :] = val


def diffusion(strip):
    row, lane = iota((E, C), 0), iota((E, C), 1)
    gy, gx = lax.axis_index("gy"), lax.axis_index("gx")
    ok_above = jnp.where(gy < lax.axis_size("gy") - 1, 1, 0)
    ok_below = jnp.where(gy > 0, 1, 0)
    ok = jnp.where(row < 64, 1, jnp.where(row < 68, ok_above, ok_below))
    if strip:
        pos = lane % 32
        ok_east = jnp.where(gx < lax.axis_size("gx") - 1, 1, 0)
        ok_west = jnp.where(gx > 0, 1, 0)
        ok = ok * jnp.where((pos >= 12) & (pos < 16), ok_east, jnp.where((pos >= 16) & (pos < 20), ok_west, 1))
    return 0.1 * ok.astype(F32)


def stage_scratch():
    return [
        pltpu.VMEM((V, E, C), F32),
        pltpu.VMEM((V, E, C), F32),
        pltpu.VMEM((V, E, C), F32),
        pltpu.VMEM((V, E, C), F32),
        pltpu.VMEM((V, E, C), F32),
        pltpu.VMEM((4, E, C), F32),
        pltpu.VMEM((4, E, C), F32),
        pltpu.VMEM((E, C), F32),
    ]


def main_stages(state, wind, below, above, third, x, f1, f2, c1, c2, w1, w2, diff):
    block = pl.program_id(0)

    @pl.when(block == 0)
    def _():
        diff[...] = diffusion(False)

    def one(k, carry):
        level = jnp.minimum(block * 8 + k, L - 1)

        def emit(v, i, val):
            third[v, k, i * 8 : i * 8 + 8, :] = val

        stage_three(f2, c2, w2, emit)
        stage_two(f1, c1, w1, f2, c2, w2)
        for v in range(V):
            for i in range(8):
                put_ring(x, v, i, state[v, k, i * 8 : i * 8 + 8, :])
            at = pl.ds((v * L + level) * 4, 4)
            put_ring(x, v, 8, jnp.concatenate([above[at, :], below[at, :]], axis=0))

        def wind_at(c, i):
            if i < 8:
                return wind[c, k, i * 8 : i * 8 + 8, :]
            at = pl.ds(BW + (c * L + level) * 3, 3)
            return jnp.concatenate([above[at, :], jnp.zeros((2, C), F32), below[at, :]], axis=0)

        stage_one(x, wind_at, diff, f1, c1, w1)
        return carry

    lax.fori_loop(0, 8, one, 0, unroll=8)


def run_main(state, wind, below, above):
    return pl.pallas_call(
        main_stages,
        grid=(5,),
        out_shape=jax.ShapeDtypeStruct((V, 40, E, C), F32),
        in_specs=[
            pl.BlockSpec((V, 8, R, C), lambda i: (0, i, 0, 0)),
            pl.BlockSpec((2, 8, R, C), lambda i: (0, i, 0, 0)),
            pl.BlockSpec((BN, C), lambda i: (0, 0)),
            pl.BlockSpec((BN, C), lambda i: (0, 0)),
        ],
        out_specs=pl.BlockSpec((V, 8, E, C), lambda i: (0, i, 0, 0)),
        scratch_shapes=stage_scratch(),
        compiler_params=pltpu.CompilerParams(vmem_limit_bytes=24 << 20),
        cost_estimate=pl.CostEstimate(flops=60_000_000, bytes_accessed=13_000_000, transcendentals=0),
        name="main_stages",
    )(state, wind, below, above)


def silu(v):
    h = 0.5 * v
    return h + h * jnp.tanh(h)


def last(*refs):
    ins, out_any, bufs = refs[:14], refs[14], refs[15:29]
    (x, f1, f2, c1, c2, w1, w2, diff, sr, zs, zx, y0, yf, b0, bm, bp, h1, h2, sems) = refs[29:]
    (strips, wstrips, fromw, frome, zone, below, above, third, forcing, land, terrain, wb, w2t, w3t) = bufs
    edge = pl.ds(BF, BN - BF)
    edges = list(ins[:5]) + [ins[5].at[edge, :], ins[6].at[edge, :]]
    done(fetch(edges, bufs[:7], sems))
    get_main = fetch(ins[7:11], bufs[7:11], sems, 7)
    get_weights = fetch(ins[11:], bufs[11:], sems, 11)
    lane = iota((8, C), 1)
    pos = lane % 32

    def unpack(p, rows, start, width):
        mine = (lane + 2 * C - start) % 32 < width
        return pltpu.roll(jnp.where(mine, frome[p, rows, :], fromw[p, rows, :]), (12 - start + C) % C, 1)

    diff[...] = diffusion(True)
    zx[0:64, :] = zone[...].astype(F32) * 0.1
    zx[64:72, :] = jnp.concatenate(
        [above[BZ - BF : BZ - BF + 1, :], jnp.zeros((6, C), F32), below[BZ - BF : BZ - BF + 1, :]], axis=0
    )
    for i in range(9):
        rows = slice(i * 8, i * 8 + 8)
        zs[rows, :] = jnp.where((pos == 19) | (pos == 12), unpack(8, rows, 8, 1), 0.0)

    in_halo = (pos >= 12) & (pos < 20)

    def strip_step(step, carry):
        lq2 = jnp.maximum(step - 2, 0)
        lq = jnp.minimum(step, LQ - 1)
        pk2 = 7 + lq2 // 8

        def emit(v, i, val):
            rows = slice(i * 8, i * 8 + 8)
            q = (lq2 % 8) * 4 + v
            sr[lq2, v, rows, :] = val + zs[rows, :] * (unpack(pk2, rows, q, 1) - val)

        stage_three(f2, c2, w2, emit)
        stage_two(f1, c1, w1, f2, c2, w2)
        pk = lq // 2
        for v in range(V):
            q4 = ((lq % 2) * 4 + v) * 4
            for i in range(9):
                rows = slice(i * 8, i * 8 + 8)
                put_ring(x, v, i, jnp.where(in_halo, unpack(pk, rows, q4, 4), strips[lq, v, rows, :]))

        def wind_at(k, i):
            rows = slice(i * 8, i * 8 + 8)
            return jnp.where(in_halo, unpack(5 + k, rows, lq * 3, 3), wstrips[lq, k, rows, :])

        stage_one(x, wind_at, diff, f1, c1, w1)
        return carry

    lax.fori_loop(0, LQ + 2, strip_step, 0, unroll=3)

    done(get_main)
    lo, hi = lane <= 2, lane >= 125

    def merge_one(v, lq, j):
        level = lq * 4 + j
        f = v * L + level
        fmain = forcing[v, level].astype(F32)
        for i in range(9):
            rows = slice(i * 8, i * 8 + 8)
            s = sr[lq, v, rows, :]
            te = pltpu.roll(s, (127 - (j * 32 + 11)) % C, 1)
            tw = pltpu.roll(s, (-(j * 32 + 20)) % C, 1)
            t = jnp.where(lo, tw, jnp.where(hi, te, third[v, level + 2, rows, :]))
            if i < 8:
                fv = fmain[i * 8 : i * 8 + 8]
            else:
                fv = jnp.concatenate(
                    [above[pl.ds(f, 1), :], jnp.zeros((6, C), F32), below[pl.ds(f, 1), :]], axis=0
                )
            r = t + zx[rows, :] * (fv - t)
            at = pl.ds((i * 8 + 1) * PITCH + f, 8, stride=PITCH)
            y0[at, :] = r
            yf[at, :] = jnp.where(lane == 127, tw, te)

    def merge(lq, carry):
        for v in range(V):
            for j in range(4):
                merge_one(v, lq, j)
        return carry

    lax.fori_loop(0, LQ - 1, merge, 0)
    for v in range(V):
        merge_one(v, LQ - 1, 0)

    def hot(yb, carry):
        lnd = land[pl.ds(yb * 8, 8), :]
        ter = terrain[pl.ds(yb * 8, 8), :]
        for k in range(8):
            j = iota((16, C), 0)
            oh = jnp.where(j < 2, jnp.where(j == lnd[k : k + 1], 1.0, 0.0), jnp.where(j - 2 == ter[k : k + 1], 1.0, 0.0))
            base = (yb * 8 + k + 1) * PITCH + F
            y0[pl.ds(base, 10), :] = oh[0:10]
            yf[pl.ds(base, 10), :] = jnp.zeros((10, C), F32)
        return carry

    lax.fori_loop(0, 8, hot, 0)
    for ref in (y0, yf):
        for p in (65, 72):
            ref[p * PITCH + F : p * PITCH + F + 10, :] = jnp.zeros((10, C), F32)
        ref[73 * PITCH : 73 * PITCH + 8, :] = jnp.zeros((8, C), F32)
        ref[66 * PITCH : 66 * PITCH + 8, :] = jnp.zeros((8, C), F32)

    def convert(p):
        src = (p if p else 72) * PITCH
        dst = p * KP
        own, outer = y0[pl.ds(src, KP), :], yf[pl.ds(src, KP), :]
        wide = iota((KP, C), 1)
        b0[pl.ds(dst, KP), :] = own.astype(BF16)
        bm[pl.ds(dst, KP), :] = pltpu.roll(jnp.where(wide == 127, outer, own), 1, 1).astype(BF16)
        bp[pl.ds(dst, KP), :] = pltpu.roll(jnp.where(wide == 0, outer, own), C - 1, 1).astype(BF16)

    for p in range(4):
        convert(p)
    done(get_weights)

    def network(t):
        if t >= 2:
            a2 = silu(h2[...]).astype(BF16)
        if 1 <= t <= R // 2:
            a1 = silu(h1[...]).astype(BF16)
        if t < R // 2:
            pairs = [
                jnp.concatenate([b[(2 * t + u) * KP : (2 * t + u + 3) * KP, :] for u in range(2)], axis=1)
                for b in (bm, b0, bp)
            ]
            acc = jnp.dot(wb[...], jnp.concatenate(pairs, axis=0), preferred_element_type=F32)
            for u in range(2):
                if 2 * t + 4 + u < 66:
                    convert(2 * t + 4 + u)
            h1[...] = acc
        if 1 <= t <= R // 2:
            h2[...] = jnp.dot(w2t[...], a1, preferred_element_type=F32)
        if t >= 2:
            ph = jnp.dot(w3t[...], a2, preferred_element_type=F32)
            for u in range(2):
                at = slice((2 * t - 3 + u) * PITCH, (2 * t - 3 + u) * PITCH + F)
                y0[at, :] = y0[at, :] + ph[:F, u * C : u * C + C]

    def put(j, v):
        rows = pl.ds(j * 8, 8)
        src = third.at[v, pl.ds(0, L), rows, :]
        return pltpu.make_async_copy(src, out_any.at[pl.ds(v * L, L), rows, :], sems.at[14 + 4 * j + v])

    def write(j):
        rows = slice(j * 8, j * 8 + 8)
        for f in range(F):
            third[f // L, f % L, rows, :] = y0[pl.ds((j * 8 + 1) * PITCH + f, 8, stride=PITCH), :]
        for v in range(V):
            put(j, v).start()

    for t in range(R // 2 + 2):
        network(t)
        if t >= 5 and t % 4 == 1:
            write((t - 5) // 4)
    for j in range(R // 8):
        for v in range(V):
            put(j, v).wait()


def run_last(*args):
    n = 74 * PITCH
    hbm = pl.BlockSpec(memory_space=pl.ANY)
    shapes = [a.shape for a in args]
    shapes[5] = shapes[6] = (BN - BF, C)
    scratch = [pltpu.VMEM(shape, a.dtype) for shape, a in zip(shapes, args)] + stage_scratch()
    scratch += [
        pltpu.VMEM((LQ, V, E, C), F32),
        pltpu.VMEM((E, C), F32),
        pltpu.VMEM((E, C), F32),
    ]
    scratch += [pltpu.VMEM((n, C), F32)] * 2 + [pltpu.VMEM((66 * KP, C), BF16)] * 3
    scratch += [
        pltpu.VMEM((256, 256), F32),
        pltpu.VMEM((256, 256), F32),
        pltpu.SemaphoreType.DMA((14 + 4 * (R // 8),)),
    ]
    return pl.pallas_call(
        last,
        out_shape=jax.ShapeDtypeStruct((F, R, C), F32),
        in_specs=[hbm] * len(args),
        out_specs=hbm,
        scratch_shapes=scratch,
        compiler_params=pltpu.CompilerParams(vmem_limit_bytes=38 << 20),
        cost_estimate=pl.CostEstimate(flops=9_000_000_000, bytes_accessed=20_000_000, transcendentals=4_000_000),
        name="strips_and_network",
    )(*args)


def local(state, wind, forcing, zone, land, terrain, first_weight, second_weight, third_weight, land_embed, terrain_embed):
    def shifts(axis):
        size = lax.axis_size(axis)
        up = [(i, i + 1) for i in range(size - 1)]
        return up, [(j, i) for i, j in up]

    down_buf, up_buf = pack_north_south(state, wind.reshape(2 * L, R, C), forcing, zone)
    up, down = shifts("gy")
    below = lax.ppermute(up_buf, "gy", up)
    above = lax.ppermute(down_buf, "gy", down)

    shaped = state.reshape(V, L, R, C)
    forced = forcing.reshape(V, L, R, C)
    packed = pack_east_west(shaped, wind, forced, zone, first_weight.transpose(0, 2, 1), land_embed.T, terrain_embed.T)
    wb = packed[4]
    strips, wstrips, east, west = pack_halo(below, above, packed[:4])
    up, down = shifts("gx")
    fromw = lax.ppermute(east, "gx", up)
    frome = lax.ppermute(west, "gx", down)
    third = run_main(shaped, wind, below, above)
    return run_last(
        strips, wstrips, fromw, frome, zone, below, above, third, forced, land, terrain, wb, second_weight, third_weight
    )


def solution(mesh):
    in_specs = (
        P(None, "gy", "gx"),
        P(None, None, "gy", "gx"),
        P(None, "gy", "gx"),
        P("gy", "gx"),
        P("gy", "gx"),
        P("gy", "gx"),
        P(),
        P(),
        P(),
        P(),
        P(),
    )
    out_specs = P(None, "gy", "gx")
    return jax.shard_map(local, mesh=mesh, in_specs=in_specs, out_specs=out_specs, check_vma=False)
```

```python
import jax
import jax.numpy as jnp
from jax import lax
from jax.experimental import pallas as pl
from jax.experimental.pallas import tpu as pltpu
from jax.sharding import PartitionSpec as P

F32, BF16 = jnp.float32, jnp.bfloat16
V, L, F, R, C = 4, 37, 148, 64, 128
LQ = 10
E = 72
BW, BF, BZ, BN = 592, 816, 964, 976
PITCH = 158
KP = 160
OFF4, OFF3, OFF1 = 4, 5, 7
THIRD = 1.0 / 3.0


def iota(shape, dim):
    return lax.broadcasted_iota(jnp.int32, shape, dim)


def ns_pack(s0, s7, w0, w7, f0, f3, z0, z7, down, up):
    for f in range(F):
        down[f * 4 : f * 4 + 4, :] = s0[f, 0:4, :]
        up[f * 4 : f * 4 + 4, :] = s7[f, 4:8, :]
    for w in range(2 * L):
        down[BW + w * 3 : BW + w * 3 + 3, :] = w0[w, 0:3, :]
        up[BW + w * 3 : BW + w * 3 + 3, :] = w7[w, 5:8, :]
    for f in range(F):
        down[BF + f : BF + f + 1, :] = f0[f].astype(F32)[0:1]
        up[BF + f : BF + f + 1, :] = f3[f].astype(F32)[15:16]
    pad = jnp.zeros((BN - BZ - 1, C), F32)
    down[BZ:BN, :] = jnp.concatenate([z0[...].astype(F32)[0:1] * 0.1, pad], axis=0)
    up[BZ:BN, :] = jnp.concatenate([z7[...].astype(F32)[7:8] * 0.1, pad], axis=0)


def pack_north_south(state, wind, forcing, zone):
    st = jax.ShapeDtypeStruct((BN, C), F32)
    full = pl.BlockSpec((BN, C), lambda i: (0, 0))
    return pl.pallas_call(
        ns_pack,
        grid=(1,),
        out_shape=(st, st),
        in_specs=[
            pl.BlockSpec((F, 8, C), lambda i: (0, 0, 0)),
            pl.BlockSpec((F, 8, C), lambda i: (0, 7, 0)),
            pl.BlockSpec((2 * L, 8, C), lambda i: (0, 0, 0)),
            pl.BlockSpec((2 * L, 8, C), lambda i: (0, 7, 0)),
            pl.BlockSpec((F, 16, C), lambda i: (0, 0, 0)),
            pl.BlockSpec((F, 16, C), lambda i: (0, 3, 0)),
            pl.BlockSpec((8, C), lambda i: (0, 0)),
            pl.BlockSpec((8, C), lambda i: (7, 0)),
        ],
        out_specs=(full, full),
        compiler_params=pltpu.CompilerParams(vmem_limit_bytes=52 << 20),
        name="ns_pack",
    )(state, state, wind, wind, forcing, forcing, zone, zone)


def selector(j, ring):
    lane = iota((C, C), 1)
    col = iota((C, C), 0)
    pos = lane % 32
    if ring:
        want = jnp.where(pos == 11, 127, jnp.where(pos == 20, 0, -1))
    else:
        want = jnp.where(pos < 12, 116 + pos, jnp.where(pos >= 20, pos - 20, -1))
    return jnp.where((want == col) & (lane // 32 == j), 1.0, 0.0).astype(BF16)


def split(x):
    hi = x.astype(BF16)
    lo = (x - hi.astype(F32)).astype(BF16)
    return hi, lo


def fill_selectors(sel, rsel):
    for j in range(4):
        one = selector(j, False)
        sel[2 * j * C : (2 * j + 1) * C, :] = one
        sel[(2 * j + 1) * C : (2 * j + 2) * C, :] = one
        rsel[j * C : (j + 1) * C, :] = selector(j, True)


def fetch(srcs, dsts, sems, first=0):
    copies = [pltpu.make_async_copy(a, b, sems.at[first + i]) for i, (a, b) in enumerate(zip(srcs, dsts))]
    for c in copies:
        c.start()
    return copies


def done(copies):
    for c in copies:
        c.wait()


def stack(parts):
    return parts[0] if len(parts) == 1 else jnp.concatenate(parts, axis=0)


def strip_of(get, keys, sel):
    wide = []
    for j in range(4):
        wide += list(split(stack([get(key, j) for key in keys])))
    return jnp.dot(jnp.concatenate(wide, axis=1), sel[...], preferred_element_type=F32)


def ring_of(get, keys, rsel):
    wide = [stack([get(key, j) for key in keys]).astype(BF16) for j in range(4)]
    return jnp.dot(jnp.concatenate(wide, axis=1), rsel[...], preferred_element_type=F32)


def zone_lanes(zed, last_column):
    to = 8 + OFF1 if last_column else 8
    only = jnp.where(iota(zed.shape, 1) == to, pltpu.roll(zed, to + 1 if last_column else to, 1), 0.0)
    tot = only
    for j in range(1, 4):
        tot = tot + pltpu.roll(only, j * 32, 1)
    return tot


def put_strips(old, width, start, parts, off):
    lane = iota(parts[0][1].shape, 1)
    for q, s in parts:
        inside = (lane + (2 * C - off) - q * width) % 32 < width
        old = jnp.where(inside, pltpu.roll(s, (q * width + off - start + C) % C, 1), old)
    return old


def prepare(first_t, land_t, terrain_t, wb):
    zero = jnp.zeros((KP - F, 256), F32)
    extra = jnp.concatenate([land_t[...].astype(F32), terrain_t[...].astype(F32), zero[:2]], axis=0)
    for b in range(3):
        tall = []
        for a in range(3):
            tall += [first_t[3 * a + b].astype(F32), extra if (a == 1 and b == 1) else zero]
        wb[:, b * 3 * KP : (b + 1) * 3 * KP] = jnp.concatenate(tall, axis=0).T.astype(BF16)


def ew_pack(state, wind, forcing, zone, first_t, land_t, terrain_t, strips, wstrips, east, west, wb, sel, rsel):
    lg = pl.program_id(0)

    @pl.when(lg == 0)
    def _():
        fill_selectors(sel, rsel)
        zed = zone[...].astype(F32) * 0.1
        for ref, at_end in ((east, True), (west, False)):
            ref[...] = jnp.zeros((9, R, C), F32)
            ref[8] = zone_lanes(zed, at_end)
        prepare(first_t, land_t, terrain_t, wb)

    def clean(x, i):
        return x if i < 5 else jnp.where(lg * 8 + i < L, x, 0.0)

    keys = [(m, v) for m in range(2) for v in range(V)]
    wkeys = [(m, c) for m in range(2) for c in range(2)]
    s = strip_of(lambda k, j: clean(state[k[1], k[0] * 4 + j], k[0] * 4 + j), keys, sel)
    f = ring_of(lambda k, j: clean(forcing[k[1], k[0] * 4 + j].astype(F32), k[0] * 4 + j), keys, rsel)
    w = strip_of(lambda k, j: clean(wind[k[1], k[0] * 4 + j], k[0] * 4 + j), wkeys, sel)
    pk = 7 + lg // 4
    for q, (m, v) in enumerate(keys):
        strips[m, v] = s[q * R : q * R + R]
    for n, (m, c) in enumerate(wkeys):
        wstrips[m, c] = w[n * R : n * R + R]
    for i in range(8):
        rows = slice(i * 8, i * 8 + 8)

        def cut(val, n):
            return val[n * R + i * 8 : n * R + i * 8 + 8]

        for ref, at4, at1, at3, on in ((east, 8, 11, 9, 1), (west, 20, 20, 20, 0)):
            ref[lg, rows, :] = put_strips(jnp.zeros((8, C), F32), 4, at4, [(q, cut(s, q)) for q in range(8)], on * OFF4)
            ref[pk, rows, :] = put_strips(
                ref[pk, rows, :], 1, at1, [((lg % 4) * 8 + q, cut(f, q)) for q in range(8)], on * OFF1
            )
            for c in range(2):
                ref[5 + c, rows, :] = put_strips(
                    ref[5 + c, rows, :], 3, at3, [(lg * 2 + m, cut(w, m * 2 + c)) for m in range(2)], on * OFF3
                )


def ew_pack_halo(below_any, above_any, s_in, w_in, e_in, x_in, strips, wstrips, east, west, sel, rsel, below, above, sems):
    get = fetch((below_any, above_any), (below, above), sems)
    fill_selectors(sel, rsel)
    done(get)
    zero = jnp.zeros((8, C), F32)

    def single(row):
        return jnp.concatenate([above[row : row + 1, :], zero[:6], below[row : row + 1, :]], axis=0)

    def four(row):
        return jnp.concatenate([above[row : row + 4, :], below[row : row + 4, :]], axis=0)

    def three(row):
        return jnp.concatenate([above[row : row + 3, :], zero[:2], below[row : row + 3, :]], axis=0)

    def state_at(k, j):
        level = k[0] * 4 + j
        return four((k[1] * L + level) * 4) if level < L else zero

    def wind_at(k, j):
        level = k[0] * 4 + j
        return three(BW + (k[1] * L + level) * 3) if level < L else zero

    def force_at(k, j):
        level = k[0] * 4 + j
        return single(BF + k[1] * L + level) if level < L else zero

    keys = [(m, v) for m in range(LQ) for v in range(V)]
    wkeys = [(m, c) for m in range(LQ) for c in range(2)]
    s = strip_of(state_at, keys, sel)
    f = ring_of(force_at, keys, rsel)
    w = strip_of(wind_at, wkeys, sel)
    zed = single(BZ)

    def cut(val, n):
        return val[n * 8 : n * 8 + 8]

    for n, (m, v) in enumerate(keys):
        strips[m, v] = cut(s, n)
    for n, (m, c) in enumerate(wkeys):
        wstrips[m, c] = cut(w, n)
    for ref, at_end, at4, at1, at3, on in ((east, True, 8, 11, 9, 1), (west, False, 20, 20, 20, 0)):
        for p in range(5):
            ref[p] = put_strips(zero, 4, at4, [(q, cut(s, p * 8 + q)) for q in range(8)], on * OFF4)
        for c in range(2):
            ref[5 + c] = put_strips(zero, 3, at3, [(m, cut(w, m * 2 + c)) for m in range(LQ)], on * OFF3)
        ref[7] = put_strips(zero, 1, at1, [(q, cut(f, q)) for q in range(32)], on * OFF1)
        ref[8] = put_strips(zone_lanes(zed, at_end), 1, at1, [(q, cut(f, 32 + q)) for q in range(8)], on * OFF1)


NS_SCRATCH = [pltpu.VMEM((BN, C), F32), pltpu.VMEM((BN, C), F32), pltpu.SemaphoreType.DMA((2,))]
SELECTORS = [pltpu.VMEM((8 * C, C), BF16), pltpu.VMEM((4 * C, C), BF16)]
PACKED = (
    jax.ShapeDtypeStruct((LQ, V, E, C), F32),
    jax.ShapeDtypeStruct((LQ, 2, E, C), F32),
    jax.ShapeDtypeStruct((9, E, C), F32),
    jax.ShapeDtypeStruct((9, E, C), F32),
)


def pack_east_west(state, wind, forcing, zone, first_t, land_t, terrain_t):
    return pl.pallas_call(
        ew_pack,
        grid=(5,),
        out_shape=PACKED + (jax.ShapeDtypeStruct((256, 9 * KP), BF16),),
        in_specs=[
            pl.BlockSpec((V, 8, R, C), lambda i: (0, i, 0, 0)),
            pl.BlockSpec((2, 8, R, C), lambda i: (0, i, 0, 0)),
            pl.BlockSpec((V, 8, R, C), lambda i: (0, i, 0, 0)),
            pl.BlockSpec((R, C), lambda i: (0, 0)),
            pl.BlockSpec(first_t.shape, lambda i: (0, 0, 0)),
            pl.BlockSpec(land_t.shape, lambda i: (0, 0)),
            pl.BlockSpec(terrain_t.shape, lambda i: (0, 0)),
        ],
        out_specs=(
            pl.BlockSpec((2, V, R, C), lambda i: (i, 0, 0, 0)),
            pl.BlockSpec((2, 2, R, C), lambda i: (i, 0, 0, 0)),
            pl.BlockSpec((9, R, C), lambda i: (0, 0, 0)),
            pl.BlockSpec((9, R, C), lambda i: (0, 0, 0)),
            pl.BlockSpec((256, 9 * KP), lambda i: (0, 0)),
        ),
        scratch_shapes=SELECTORS,
        compiler_params=pltpu.CompilerParams(vmem_limit_bytes=32 << 20),
        cost_estimate=pl.CostEstimate(flops=4_000_000_000, bytes_accessed=13_000_000, transcendentals=0),
        name="ew_pack",
    )(state, wind, forcing, zone, first_t, land_t, terrain_t)


def pack_halo(below, above, packed):
    hbm = pl.BlockSpec(memory_space=pl.ANY)
    return pl.pallas_call(
        ew_pack_halo,
        grid=(1,),
        out_shape=PACKED,
        in_specs=[hbm] * 6,
        out_specs=(
            pl.BlockSpec((LQ, V, 8, C), lambda i: (0, 0, 8, 0)),
            pl.BlockSpec((LQ, 2, 8, C), lambda i: (0, 0, 8, 0)),
            pl.BlockSpec((9, 8, C), lambda i: (0, 8, 0)),
            pl.BlockSpec((9, 8, C), lambda i: (0, 8, 0)),
        ),
        scratch_shapes=SELECTORS + NS_SCRATCH,
        input_output_aliases={2: 0, 3: 1, 4: 2, 5: 3},
        compiler_params=pltpu.CompilerParams(vmem_limit_bytes=24 << 20),
        name="ew_pack_halo",
    )(below, above, *packed)


def put_ring(ref, v, i, val):
    ref[v, i * 8 : i * 8 + 8, :] = val


class Around:
    def __init__(self, ref):
        self.ref, self.have = ref, {}
        row = iota((8, C), 0)
        self.top, self.bottom = row == 7, row == 0

    def block(self, v, i):
        i = i % 9 + (9 if i == 9 else 0)
        if (v, i) not in self.have:
            k = i % 9
            q = self.ref[v, k * 8 : k * 8 + 8, :]
            self.have[v, i] = (q, pltpu.roll(q, 7, 0), pltpu.roll(q, 1, 0))
        return self.have[v, i]

    def __call__(self, v, i):
        if i == 0:
            q8 = self.ref[v, 64:72, :]
            before = pltpu.roll(q8, 1, 0)
        else:
            before = self.block(v, i - 1)[2]
        q, up, dn = self.block(v, i)
        n = jnp.where(self.top, self.block(v, i + 1)[1], up)
        s = jnp.where(self.bottom, before, dn)
        return q, pltpu.roll(q, C - 1, 1), pltpu.roll(q, 1, 1), n, s


def stage_three(f2, c2, w2, emit):
    at = Around(f2)
    for i in range(9):
        rows = slice(i * 8, i * 8 + 8)
        ce, cw, cn, cs = (w2[k, rows, :] for k in range(4))
        for v in range(V):
            q, e, w, n, s = at(v, i)
            g = (ce * e + cw * w) + (cn * n + cs * s)
            emit(v, i, THIRD * c2[v, rows, :] + (2.0 * THIRD) * (0.6 * q + g))


def stage_two(f1, c1, w1, f2, c2, w2):
    at = Around(f1)
    for i in range(9):
        rows = slice(i * 8, i * 8 + 8)
        ce, cw, cn, cs = (w1[k, rows, :] for k in range(4))
        for v in range(V):
            q, e, w, n, s = at(v, i)
            g = (ce * e + cw * w) + (cn * n + cs * s)
            c = c1[v, rows, :]
            c2[v, rows, :] = c
            put_ring(f2, v, i, 0.75 * c + 0.25 * (0.6 * q + g))
        for k, val in enumerate((ce, cw, cn, cs)):
            w2[k, rows, :] = val


def stage_one(x, wind_at, diff, f1, c1, w1):
    at = Around(x)
    for i in range(9):
        rows = slice(i * 8, i * 8 + 8)
        d = diff[rows, :]
        hu, hv = (0.5 * wind_at(k, i) for k in range(2))
        ce, cw, cn, cs = d - hu, d + hu, d - hv, d + hv
        for v in range(V):
            q, e, w, n, s = at(v, i)
            g = (ce * e + cw * w) + (cn * n + cs * s)
            c1[v, rows, :] = q
            put_ring(f1, v, i, 0.6 * q + g)
        for k, val in enumerate((ce, cw, cn, cs)):
            w1[k, rows, :] = val


def diffusion(strip):
    row, lane = iota((E, C), 0), iota((E, C), 1)
    gy, gx = lax.axis_index("gy"), lax.axis_index("gx")
    ok_above = jnp.where(gy < lax.axis_size("gy") - 1, 1, 0)
    ok_below = jnp.where(gy > 0, 1, 0)
    ok = jnp.where(row < 64, 1, jnp.where(row < 68, ok_above, ok_below))
    if strip:
        pos = lane % 32
        ok_east = jnp.where(gx < lax.axis_size("gx") - 1, 1, 0)
        ok_west = jnp.where(gx > 0, 1, 0)
        ok = ok * jnp.where((pos >= 12) & (pos < 16), ok_east, jnp.where((pos >= 16) & (pos < 20), ok_west, 1))
    return 0.1 * ok.astype(F32)


def stage_scratch():
    return [
        pltpu.VMEM((V, E, C), F32),
        pltpu.VMEM((V, E, C), F32),
        pltpu.VMEM((V, E, C), F32),
        pltpu.VMEM((V, E, C), F32),
        pltpu.VMEM((V, E, C), F32),
        pltpu.VMEM((4, E, C), F32),
        pltpu.VMEM((4, E, C), F32),
        pltpu.VMEM((E, C), F32),
    ]


def main_stages(state, wind, below, above, third, x, f1, f2, c1, c2, w1, w2, diff):
    block = pl.program_id(0)

    @pl.when(block == 0)
    def _():
        diff[...] = diffusion(False)

    def one(k, carry):
        level = jnp.minimum(block * 8 + k, L - 1)

        def emit(v, i, val):
            third[v, k, i * 8 : i * 8 + 8, :] = val

        stage_three(f2, c2, w2, emit)
        stage_two(f1, c1, w1, f2, c2, w2)
        for v in range(V):
            for i in range(8):
                put_ring(x, v, i, state[v, k, i * 8 : i * 8 + 8, :])
            at = pl.ds((v * L + level) * 4, 4)
            put_ring(x, v, 8, jnp.concatenate([above[at, :], below[at, :]], axis=0))

        def wind_at(c, i):
            if i < 8:
                return wind[c, k, i * 8 : i * 8 + 8, :]
            at = pl.ds(BW + (c * L + level) * 3, 3)
            return jnp.concatenate([above[at, :], jnp.zeros((2, C), F32), below[at, :]], axis=0)

        stage_one(x, wind_at, diff, f1, c1, w1)
        return carry

    lax.fori_loop(0, 8, one, 0, unroll=8)


def run_main(state, wind, below, above):
    return pl.pallas_call(
        main_stages,
        grid=(5,),
        out_shape=jax.ShapeDtypeStruct((V, 40, E, C), F32),
        in_specs=[
            pl.BlockSpec((V, 8, R, C), lambda i: (0, i, 0, 0)),
            pl.BlockSpec((2, 8, R, C), lambda i: (0, i, 0, 0)),
            pl.BlockSpec((BN, C), lambda i: (0, 0)),
            pl.BlockSpec((BN, C), lambda i: (0, 0)),
        ],
        out_specs=pl.BlockSpec((V, 8, E, C), lambda i: (0, i, 0, 0)),
        scratch_shapes=stage_scratch(),
        compiler_params=pltpu.CompilerParams(vmem_limit_bytes=24 << 20),
        cost_estimate=pl.CostEstimate(flops=60_000_000, bytes_accessed=13_000_000, transcendentals=0),
        name="main_stages",
    )(state, wind, below, above)


def silu(v):
    h = 0.5 * v
    return h + h * jnp.tanh(h)


def last(*refs):
    ins, out_any, bufs = refs[:14], refs[14], refs[15:29]
    (x, f1, f2, c1, c2, w1, w2, diff, sr, zs, zx, y0, yf, b0, bm, bp, h1, h2, sems) = refs[29:]
    (strips, wstrips, fromw, frome, zone, below, above, third, forcing, land, terrain, wb, w2t, w3t) = bufs
    edge = pl.ds(BF, BN - BF)
    edges = list(ins[:5]) + [ins[5].at[edge, :], ins[6].at[edge, :]]
    done(fetch(edges, bufs[:7], sems))
    get_main = fetch(ins[7:11], bufs[7:11], sems, 7)
    get_weights = fetch(ins[11:], bufs[11:], sems, 11)
    lane = iota((8, C), 1)
    pos = lane % 32

    def unpack(p, rows, start, width):
        mine = (lane + 2 * C - start) % 32 < width
        return pltpu.roll(jnp.where(mine, frome[p, rows, :], fromw[p, rows, :]), (12 - start + C) % C, 1)

    diff[...] = diffusion(True)
    zx[0:64, :] = zone[...].astype(F32) * 0.1
    zx[64:72, :] = jnp.concatenate(
        [above[BZ - BF : BZ - BF + 1, :], jnp.zeros((6, C), F32), below[BZ - BF : BZ - BF + 1, :]], axis=0
    )
    for i in range(9):
        rows = slice(i * 8, i * 8 + 8)
        zs[rows, :] = jnp.where((pos == 19) | (pos == 12), unpack(8, rows, 8, 1), 0.0)

    in_halo = (pos >= 12) & (pos < 20)

    def strip_step(step, carry):
        lq2 = jnp.maximum(step - 2, 0)
        lq = jnp.minimum(step, LQ - 1)
        pk2 = 7 + lq2 // 8

        def emit(v, i, val):
            rows = slice(i * 8, i * 8 + 8)
            q = (lq2 % 8) * 4 + v
            sr[lq2, v, rows, :] = val + zs[rows, :] * (unpack(pk2, rows, q, 1) - val)

        stage_three(f2, c2, w2, emit)
        stage_two(f1, c1, w1, f2, c2, w2)
        pk = lq // 2
        for v in range(V):
            q4 = ((lq % 2) * 4 + v) * 4
            for i in range(9):
                rows = slice(i * 8, i * 8 + 8)
                put_ring(x, v, i, jnp.where(in_halo, unpack(pk, rows, q4, 4), strips[lq, v, rows, :]))

        def wind_at(k, i):
            rows = slice(i * 8, i * 8 + 8)
            return jnp.where(in_halo, unpack(5 + k, rows, lq * 3, 3), wstrips[lq, k, rows, :])

        stage_one(x, wind_at, diff, f1, c1, w1)
        return carry

    lax.fori_loop(0, LQ + 2, strip_step, 0, unroll=6)

    done(get_main)
    lo, hi = lane <= 2, lane >= 125

    def merge_one(v, lq, j):
        level = lq * 4 + j
        f = v * L + level
        fmain = forcing[v, level].astype(F32)
        for i in range(9):
            rows = slice(i * 8, i * 8 + 8)
            s = sr[lq, v, rows, :]
            te = pltpu.roll(s, (127 - (j * 32 + 11)) % C, 1)
            tw = pltpu.roll(s, (-(j * 32 + 20)) % C, 1)
            t = jnp.where(lo, tw, jnp.where(hi, te, third[v, level + 2, rows, :]))
            if i < 8:
                fv = fmain[i * 8 : i * 8 + 8]
            else:
                fv = jnp.concatenate(
                    [above[pl.ds(f, 1), :], jnp.zeros((6, C), F32), below[pl.ds(f, 1), :]], axis=0
                )
            r = t + zx[rows, :] * (fv - t)
            at = pl.ds((i * 8 + 1) * PITCH + f, 8, stride=PITCH)
            y0[at, :] = r
            yf[at, :] = jnp.where(lane == 127, tw, te)

    def merge(lq, carry):
        for v in range(V):
            for j in range(4):
                merge_one(v, lq, j)
        return carry

    lax.fori_loop(0, LQ - 1, merge, 0, unroll=3)
    for v in range(V):
        merge_one(v, LQ - 1, 0)

    def hot(yb, carry):
        lnd = land[pl.ds(yb * 8, 8), :]
        ter = terrain[pl.ds(yb * 8, 8), :]
        for k in range(8):
            j = iota((16, C), 0)
            oh = jnp.where(j < 2, jnp.where(j == lnd[k : k + 1], 1.0, 0.0), jnp.where(j - 2 == ter[k : k + 1], 1.0, 0.0))
            base = (yb * 8 + k + 1) * PITCH + F
            y0[pl.ds(base, 10), :] = oh[0:10]
            yf[pl.ds(base, 10), :] = jnp.zeros((10, C), F32)
        return carry

    lax.fori_loop(0, 8, hot, 0)
    for ref in (y0, yf):
        for p in (65, 72):
            ref[p * PITCH + F : p * PITCH + F + 10, :] = jnp.zeros((10, C), F32)
        ref[73 * PITCH : 73 * PITCH + 8, :] = jnp.zeros((8, C), F32)
        ref[66 * PITCH : 66 * PITCH + 8, :] = jnp.zeros((8, C), F32)

    def convert(p):
        src = (p if p else 72) * PITCH
        dst = p * KP
        own, outer = y0[pl.ds(src, KP), :], yf[pl.ds(src, KP), :]
        wide = iota((KP, C), 1)
        b0[pl.ds(dst, KP), :] = own.astype(BF16)
        bm[pl.ds(dst, KP), :] = pltpu.roll(jnp.where(wide == 127, outer, own), 1, 1).astype(BF16)
        bp[pl.ds(dst, KP), :] = pltpu.roll(jnp.where(wide == 0, outer, own), C - 1, 1).astype(BF16)

    for p in range(4):
        convert(p)
    done(get_weights)

    def network(t):
        if t >= 2:
            a2 = silu(h2[...]).astype(BF16)
        if 1 <= t <= R // 2:
            a1 = silu(h1[...]).astype(BF16)
        if t < R // 2:
            pairs = [
                jnp.concatenate([b[(2 * t + u) * KP : (2 * t + u + 3) * KP, :] for u in range(2)], axis=1)
                for b in (bm, b0, bp)
            ]
            acc = jnp.dot(wb[...], jnp.concatenate(pairs, axis=0), preferred_element_type=F32)
            for u in range(2):
                if 2 * t + 4 + u < 66:
                    convert(2 * t + 4 + u)
            h1[...] = acc
        if 1 <= t <= R // 2:
            h2[...] = jnp.dot(w2t[...], a1, preferred_element_type=F32)
        if t >= 2:
            ph = jnp.dot(w3t[...], a2, preferred_element_type=F32)
            for u in range(2):
                at = slice((2 * t - 3 + u) * PITCH, (2 * t - 3 + u) * PITCH + F)
                y0[at, :] = y0[at, :] + ph[:F, u * C : u * C + C]

    def put(j, v):
        rows = pl.ds(j * 8, 8)
        src = third.at[v, pl.ds(0, L), rows, :]
        return pltpu.make_async_copy(src, out_any.at[pl.ds(v * L, L), rows, :], sems.at[14 + 4 * j + v])

    def write(j):
        rows = slice(j * 8, j * 8 + 8)
        for f in range(F):
            third[f // L, f % L, rows, :] = y0[pl.ds((j * 8 + 1) * PITCH + f, 8, stride=PITCH), :]
        for v in range(V):
            put(j, v).start()

    for t in range(R // 2 + 2):
        network(t)
        if t >= 5 and t % 4 == 1:
            write((t - 5) // 4)
    for j in range(R // 8):
        for v in range(V):
            put(j, v).wait()


def run_last(*args):
    n = 74 * PITCH
    hbm = pl.BlockSpec(memory_space=pl.ANY)
    shapes = [a.shape for a in args]
    shapes[5] = shapes[6] = (BN - BF, C)
    scratch = [pltpu.VMEM(shape, a.dtype) for shape, a in zip(shapes, args)] + stage_scratch()
    scratch += [
        pltpu.VMEM((LQ, V, E, C), F32),
        pltpu.VMEM((E, C), F32),
        pltpu.VMEM((E, C), F32),
    ]
    scratch += [pltpu.VMEM((n, C), F32)] * 2 + [pltpu.VMEM((66 * KP, C), BF16)] * 3
    scratch += [
        pltpu.VMEM((256, 256), F32),
        pltpu.VMEM((256, 256), F32),
        pltpu.SemaphoreType.DMA((14 + 4 * (R // 8),)),
    ]
    return pl.pallas_call(
        last,
        out_shape=jax.ShapeDtypeStruct((F, R, C), F32),
        in_specs=[hbm] * len(args),
        out_specs=hbm,
        scratch_shapes=scratch,
        compiler_params=pltpu.CompilerParams(vmem_limit_bytes=38 << 20),
        cost_estimate=pl.CostEstimate(flops=9_000_000_000, bytes_accessed=20_000_000, transcendentals=4_000_000),
        name="strips_and_network",
    )(*args)


def local(state, wind, forcing, zone, land, terrain, first_weight, second_weight, third_weight, land_embed, terrain_embed):
    def shifts(axis):
        size = lax.axis_size(axis)
        up = [(i, i + 1) for i in range(size - 1)]
        return up, [(j, i) for i, j in up]

    down_buf, up_buf = pack_north_south(state, wind.reshape(2 * L, R, C), forcing, zone)
    up, down = shifts("gy")
    below = lax.ppermute(up_buf, "gy", up)
    above = lax.ppermute(down_buf, "gy", down)

    shaped = state.reshape(V, L, R, C)
    forced = forcing.reshape(V, L, R, C)
    packed = pack_east_west(shaped, wind, forced, zone, first_weight.transpose(0, 2, 1), land_embed.T, terrain_embed.T)
    wb = packed[4]
    strips, wstrips, east, west = pack_halo(below, above, packed[:4])
    up, down = shifts("gx")
    fromw = lax.ppermute(east, "gx", up)
    frome = lax.ppermute(west, "gx", down)
    third = run_main(shaped, wind, below, above)
    return run_last(
        strips, wstrips, fromw, frome, zone, below, above, third, forced, land, terrain, wb, second_weight, third_weight
    )


def solution(mesh):
    in_specs = (
        P(None, "gy", "gx"),
        P(None, None, "gy", "gx"),
        P(None, "gy", "gx"),
        P("gy", "gx"),
        P("gy", "gx"),
        P("gy", "gx"),
        P(),
        P(),
        P(),
        P(),
        P(),
    )
    out_specs = P(None, "gy", "gx")
    return jax.shard_map(local, mesh=mesh, in_specs=in_specs, out_specs=out_specs, check_vma=False)
```
